512 devices in a mesh: clip: 32 (over z, x_lo, core), sp: 16 (over y, x_hi).
Axes of the slice: x: 4 (x_hi: 2, x_lo: 2; x = x_hi * 2 + x_lo), y: 8, z: 8, core: 2. Of those that a mesh axis runs over, the one named last changes fastest.
Arguments:
- features: bfloat16 [2, 3, 32, 4, 128, 2048], P(None, None, 'clip', None, 'sp'), may hold values from -6 to 6, as said below
- context: bfloat16 [32, 2, 64, 2048], P('clip', None, None, 'sp'), may hold values from -6 to 6
- scene_cuts: int32 [32], replicated, may hold values 0 or 1
- key_clips: int32 [4], replicated, may hold values from 0 to 31, as said below
- owner_slot: int32 [32, 2], P('clip'), may hold values from 0 to 3
Outputs:
- mixed: bfloat16 [2, 32, 4, 128, 2048], P(None, 'clip', None, 'sp')
The draws below stay inside these ranges and needn't reach their ends.
Inputs may be any that keep to these rules, and one draw needn't show every extreme that they name: `features`: keys and values lie within the range; queries too. `key_clips`: 4 distinct clips; clip 0 and clip 32 - 1 are always among them.
All inputs are finite; a program needn't handle non-finite values.
Results may differ from the reference program's by a relative error of at most 0.0042.
Values may be sent and summed in bfloat16 or wider, within the bound.
A program may use at most 64 MiB of HBM per device.

```python
import jax
import jax.numpy as jnp
from jax import lax

HEADS = 32
HEAD_DIM = 64
FRAMES = 4
POOL = 2
NOWN = 2
NKEY = 4
CLIPS = 32
SPATIAL = 128
CTX = 64


def draw_features(key, part):
    key = jax.random.fold_in(key, 11)
    shape = (2, 3, CLIPS, FRAMES, SPATIAL, HEADS * HEAD_DIM)
    key_base = jax.random.fold_in(key, 0)
    spread = jnp.array([1.6, 1.6, 1.0], jnp.float32).reshape(1, 3, 1, 1, 1, 1)
    base = jnp.clip(jax.random.normal(key_base, shape, jnp.float32) * spread, -6.0, 6.0)
    return base.astype(jnp.bfloat16)


def draw_key_clips(key, part):
    key = jax.random.fold_in(key, 23)
    middle = jax.random.permutation(key, CLIPS - 2) + 1
    return jnp.concatenate([jnp.zeros((1,), jnp.int32), middle[:NKEY - 2].astype(jnp.int32), jnp.full((1,), CLIPS - 1, jnp.int32)])


def plant(entries, rng, least, top_value):
    dims = entries.shape
    spot = [jax.random.randint(jax.random.fold_in(rng, axis), (), 0, dims[axis]) for axis in range(len(dims))]
    entries = entries.at[tuple(spot)].set(least)
    longest = dims.index(max(dims))
    spot[longest] = (spot[longest] + 1) % dims[longest]
    return entries.at[tuple(spot)].set(top_value)


def levels(own_key, extent, pieces, low, largest):
    gain = 1.0
    for dim, blocks in pieces:
        draws = jax.random.uniform(jax.random.fold_in(jax.random.fold_in(own_key, 6), dim), (blocks,), jnp.float32, low / len(pieces), largest / len(pieces))
        gain = gain * jnp.repeat(jnp.exp(draws), extent[dim] // blocks).reshape((-1,) + (1,) * (len(extent) - 1 - dim))
    return gain


def scatter_about(key, dims, deviation, most, cuts=(), kind=jnp.bfloat16):
    drawn = jax.random.normal(key, dims, jnp.float32) * deviation
    if len(cuts) > 0:
        drawn = levels(key, dims, cuts, -0.22, 0.18) * drawn
    return jnp.clip(drawn, min=-most, max=most).astype(kind)


def setup_inputs(seed: int = 0) -> dict:
    keys = jax.random.split(jax.random.key(seed), 6)
    return {
        "features": draw_features(jax.random.fold_in(keys[5], 71), 0),
        "context": scatter_about(keys[1], (CLIPS, 2, CTX, HEADS * HEAD_DIM), 1.6, 6.0, ((0, 32), (3, 16))),
        "scene_cuts": plant((jax.random.randint(keys[2], (CLIPS,), 0, 4) < 1).astype(jnp.int32), jax.random.fold_in(keys[2], 1), 0, 1),
        "key_clips": draw_key_clips(jax.random.fold_in(keys[5], 71), 0),
        "owner_slot": plant(jax.random.randint(keys[4], (CLIPS, NOWN), 0, NKEY), jax.random.fold_in(keys[4], 1), 0, NKEY - 1).astype(jnp.int32),
    }


NEG_FILL = -1e30


def attend_head(queries, all_keys, all_values, usable, scaling):
    scores = jnp.dot(queries, all_keys.T, preferred_element_type=jnp.float32) * scaling
    scores = jnp.where(usable[None, :], scores, NEG_FILL)
    top_score = jnp.max(scores, axis=1, keepdims=True)
    weights = jnp.exp(scores - top_score)
    total = jnp.sum(weights, axis=1, keepdims=True)
    rounded = weights.astype(jnp.bfloat16)
    summed = jnp.dot(rounded, all_values, preferred_element_type=jnp.float32)
    return (summed / total).astype(jnp.bfloat16)


def reference(features, context, scene_cuts, key_clips, owner_slot):
    lane_count = HEADS * HEAD_DIM
    scaling = HEAD_DIM ** -0.5
    clip_ids = jnp.arange(CLIPS, dtype=jnp.int32)
    cuts_after = jnp.concatenate([scene_cuts[1:], jnp.ones((1,), jnp.int32)])
    before_ok = (clip_ids > 0) & (scene_cuts == 0)
    after_ok = (clip_ids < CLIPS - 1) & (cuts_after == 0)
    owners = key_clips[owner_slot]
    first_pair = features[0, 1:3]
    zero_frame = jnp.zeros((2, 1, SPATIAL, lane_count), jnp.bfloat16)
    before = jnp.concatenate([zero_frame, first_pair[:, :-1, FRAMES - 1]], axis=1)
    after = jnp.concatenate([first_pair[:, 1:, 0], zero_frame], axis=1)
    pooled = first_pair[:, :, 0].astype(jnp.float32).reshape(2, CLIPS, CTX, POOL, lane_count).sum(axis=3) * (POOL ** -0.5)
    pooled = jnp.transpose(pooled.astype(jnp.bfloat16), (1, 0, 2, 3))
    results = []
    for step_index, context_now in ((0, context), (1, pooled)):
        chosen = context_now[owners]

        def one_clip(items):
            queries, own_keys, own_values, key_before, value_before, key_after, value_after, picked, ok_before, ok_after = items
            all_keys = jnp.concatenate([own_keys.reshape(-1, lane_count), key_before, key_after, picked[:, 0].reshape(-1, lane_count)])
            all_values = jnp.concatenate([own_values.reshape(-1, lane_count), value_before, value_after, picked[:, 1].reshape(-1, lane_count)])
            usable = jnp.concatenate([
                jnp.ones((FRAMES * SPATIAL,), jnp.bool_),
                jnp.broadcast_to(ok_before, (SPATIAL,)),
                jnp.broadcast_to(ok_after, (SPATIAL,)),
                jnp.ones((NOWN * CTX,), jnp.bool_)])
            head_queries = queries.reshape(-1, HEADS, HEAD_DIM).transpose(1, 0, 2)
            head_keys = all_keys.reshape(-1, HEADS, HEAD_DIM).transpose(1, 0, 2)
            head_values = all_values.reshape(-1, HEADS, HEAD_DIM).transpose(1, 0, 2)
            per_head = lax.map(lambda trio: attend_head(trio[0], trio[1], trio[2], usable, scaling), (head_queries, head_keys, head_values))
            return per_head.transpose(1, 0, 2).reshape(FRAMES, SPATIAL, lane_count)

        results.append(lax.map(one_clip, (features[step_index, 0], features[step_index, 1], features[step_index, 2],
                                          before[0], before[1], after[0], after[1], chosen, before_ok, after_ok)))
    return jnp.stack(results)
```

```python
import functools

import jax
import jax.numpy as jnp
from jax import lax
from jax.experimental import pallas as pl
from jax.experimental.pallas import tpu as pltpu
from jax.sharding import PartitionSpec as P

HEAD_DIM = 64
LANES = 128
QUAD = 4
MESH = pl.DeviceIdType.MESH


def wait_bytes(ref, sem):
    pltpu.make_async_copy(ref, ref, sem).wait()


def flat(block):
    wide = block.astype(jnp.float32)
    return wide.reshape(-1, LANES).astype(jnp.bfloat16)


def kernel(
    clips,
    sps,
    feat,
    ctx,
    cuts,
    key_clips,
    slots,
    out,
    recv,
    edge,
    pooled,
    scat_0,
    scat_1,
    pick,
    quad_0,
    quad_1,
    full_0,
    full_1,
    keys,
    vals,
    done,
    in_send,
    in_recv,
    own_sem,
    edge_send,
    edge_recv,
    ex_send,
    ex_recv,
    out_send,
    out_recv,
):
    c = lax.axis_index("clip")
    s = lax.axis_index("sp")
    zs = clips // QUAD
    z = c // QUAD
    q = c % QUAD
    frames = recv.shape[2]
    tiles = ctx.shape[0]
    part = tiles // zs
    frame_rows = sps * 8
    own_rows = frames * frame_rows
    ctx_rows = tiles * 4
    scat, quad, full = (scat_0, scat_1), (quad_0, quad_1), (full_0, full_1)

    barrier = pltpu.get_barrier_semaphore()

    def greet(clip, sp):
        pl.semaphore_signal(barrier, inc=1, device_id=(clip, sp), device_id_type=MESH)

    def greet_sp(k, _):
        greet(c, (s + k) % sps)
        return 0

    def greet_z(k, _):
        greet(((z + k) % zs) * QUAD + q, s)
        return 0

    def greet_quad(k, _):
        greet(z * QUAD + (q + k) % QUAD, s)
        return 0

    before = (c + clips - 1) % clips
    after = (c + 1) % clips
    lax.fori_loop(1, sps, greet_sp, 0)
    lax.fori_loop(1, zs, greet_z, 0)
    lax.fori_loop(1, QUAD, greet_quad, 0)
    greet(before, s)
    greet(after, s)
    pl.semaphore_wait(barrier, sps - 1 + zs - 1 + QUAD - 1 + 2)

    def remote(src, dst, send, rcv, clip, sp):
        pltpu.make_async_remote_copy(
            src_ref=src,
            dst_ref=dst,
            send_sem=send,
            recv_sem=rcv,
            device_id=(clip, sp),
            device_id_type=MESH,
        ).start()

    groups = ((0, 1, 2), (0, 0, 1), (1, 0, 3))

    def block(ref, group, sp):
        step, low, size = group
        return ref.at[step, pl.ds(low, size), :, :, pl.ds(sp * LANES, LANES)]

    def place(group, sp):
        step, low, size = group
        return recv.at[step, pl.ds(low, size), :, sp]

    def send_group(g):
        group = groups[g]

        def one(k, _):
            to = (s + k) % sps
            remote(block(feat, group, to), place(group, s), in_send.at[g], in_recv.at[g], c, to)
            return 0

        pltpu.make_async_copy(block(feat, group, s), place(group, s), own_sem.at[g]).start()
        lax.fori_loop(1, sps, one, 0)

    def others(group):
        step, low, size = group
        return recv.at[step, pl.ds(low, size), :, pl.ds(0, sps - 1)]

    def wait_group(g):
        pltpu.make_async_copy(block(feat, groups[g], s), place(groups[g], s), own_sem.at[g]).wait()
        wait_bytes(others(groups[g]), in_recv.at[g])

    def scatter(e, src):
        def one(k, _):
            to = (z + k) % zs
            remote(
                src.at[pl.ds(to * part, part)],
                scat[e].at[z],
                ex_send.at[e, 0],
                ex_recv.at[e, 0],
                to * QUAD + q,
                s,
            )
            return 0

        lax.fori_loop(1, zs, one, 0)
        own = pltpu.make_async_copy(src.at[pl.ds(z * part, part)], scat[e].at[z], own_sem.at[3 + e])
        own.start()
        own.wait()

    def exchange(e):
        wait_bytes(scat[e].at[pl.ds(0, zs - 1)], ex_recv.at[e, 0])
        for i in range(QUAD):
            pick[e, i] = scat[e][key_clips[i] // QUAD]

        def one(k, _):
            remote(
                pick.at[e],
                quad[e].at[q],
                ex_send.at[e, 1],
                ex_recv.at[e, 1],
                z * QUAD + (q + k) % QUAD,
                s,
            )
            return 0

        lax.fori_loop(1, QUAD, one, 0)
        quad[e][q] = pick[e]

    def gather(e):
        wait_bytes(quad[e].at[pl.ds(0, QUAD - 1)], ex_recv.at[e, 1])
        for i in range(QUAD):
            full[e][z, i] = quad[e][key_clips[i] % QUAD, i]

        def one(k, _):
            remote(
                full[e].at[z],
                full[e].at[z],
                ex_send.at[e, 2],
                ex_recv.at[e, 2],
                ((z + k) % zs) * QUAD + q,
                s,
            )
            return 0

        lax.fori_loop(1, zs, one, 0)

    scatter(0, ctx)
    send_group(0)
    send_group(1)
    send_group(2)
    exchange(0)
    gather(0)

    wait_group(0)
    remote(recv.at[0, pl.ds(1, 2), frames - 1], edge.at[0], edge_send.at[0], edge_recv.at[0], after, s)
    remote(recv.at[0, pl.ds(1, 2), 0], edge.at[1], edge_send.at[1], edge_recv.at[1], before, s)
    half = tiles // 2
    row = lax.broadcasted_iota(jnp.int32, (half * 8, frame_rows), 0)
    col = lax.broadcasted_iota(jnp.int32, (half * 8, frame_rows), 1)
    pairs = ((col == 2 * row) | (col == 2 * row + 1)).astype(jnp.bfloat16)
    for j in range(2):
        added = jnp.dot(pairs, flat(recv[0, 1 + j, 0]), preferred_element_type=jnp.float32)
        pooled[pl.ds(j * half, half)] = (added * 2**-0.5).reshape(half, 8, LANES).astype(jnp.bfloat16)
    scatter(1, pooled)

    before_ok = (c > 0) & (cuts[c] == 0)
    after_ok = (c < clips - 1) & (cuts[after] == 0)
    lane = lax.broadcasted_iota(jnp.int32, (1, LANES), 1)
    first = lane < HEAD_DIM

    def put(step, base, key_rows, value_rows, ok=None):
        rows = key_rows.shape[0]
        where = pl.ds(base, rows)
        ones = jnp.ones((rows, LANES), jnp.float32)
        value_rows = value_rows.astype(jnp.float32)
        if ok is not None:
            value_rows = jnp.where(ok, value_rows, 0.0)
            ones = jnp.where(ok, ones, 0.0)
        keys[step, where] = key_rows
        vals[step, 0, where] = jnp.where(first, value_rows, ones).astype(jnp.bfloat16)
        vals[step, 1, where] = jnp.where(first, ones, value_rows).astype(jnp.bfloat16)

    def put_own(step):
        for f in range(frames):
            put(step, f * frame_rows, flat(recv[step, 1, f]), flat(recv[step, 2, f]))

    def put_edge(step):
        for side, ok in ((0, before_ok), (1, after_ok)):
            own = recv[step, 1, 0].astype(jnp.float32)
            key_rows = jnp.where(ok, edge[side, 0].astype(jnp.float32), own)
            key_rows = key_rows.reshape(-1, LANES).astype(jnp.bfloat16)
            put(step, own_rows + side * frame_rows, key_rows, flat(edge[side, 1]), ok)

    def put_context(step):
        wait_bytes(full[step].at[pl.ds(0, zs - 1)], ex_recv.at[step, 2])
        for i in range(2):
            base = own_rows + 2 * frame_rows + i * ctx_rows
            taken = flat(full[step][:, slots[i]])
            put(step, base, taken[:ctx_rows], taken[ctx_rows:])

    def attend(step, f):
        queries = flat(recv[step, 0, f]).astype(jnp.float32) * HEAD_DIM**-0.5
        both = jnp.concatenate(
            [jnp.where(first, queries, 0.0), jnp.where(first, 0.0, queries)], axis=0
        ).astype(jnp.bfloat16)
        scores = lax.dot_general(
            both, keys[step], (((1,), (1,)), ((), ())), preferred_element_type=jnp.float32
        )
        top = jnp.max(scores, axis=1, keepdims=True)
        weights = jnp.exp(scores - top).astype(jnp.bfloat16)
        left = jnp.dot(weights[:frame_rows], vals[step, 0], preferred_element_type=jnp.float32)
        right = jnp.dot(weights[frame_rows:], vals[step, 1], preferred_element_type=jnp.float32)
        numer = jnp.where(first, left, right)
        total = pltpu.roll(jnp.where(first, right, left), HEAD_DIM, 1)
        done[step, f] = (numer / total).reshape(sps, 8, LANES).astype(jnp.bfloat16)

    def send_out(step):
        def one(k, _):
            to = (s + k) % sps
            remote(
                done.at[step, :, to],
                out.at[step, :, :, pl.ds(s * LANES, LANES)],
                out_send.at[step],
                out_recv.at[step],
                c,
                to,
            )
            return 0

        lax.fori_loop(1, sps, one, 0)
        pltpu.make_async_copy(
            done.at[step, :, s], out.at[step, :, :, pl.ds(s * LANES, LANES)], own_sem.at[5 + step]
        ).start()

    put_own(0)
    exchange(1)
    wait_group(1)
    wait_bytes(edge.at[0], edge_recv.at[0])
    wait_bytes(edge.at[1], edge_recv.at[1])
    put_edge(0)
    put_context(0)
    for f in range(frames):
        attend(0, f)
        if f == 0:
            gather(1)
    send_out(0)

    wait_group(2)
    put_own(1)
    put_edge(1)
    put_context(1)
    for f in range(frames):
        attend(1, f)
    send_out(1)

    for g in range(3):
        wait_bytes(others(groups[g]), in_send.at[g])
    for side in range(2):
        wait_bytes(edge.at[side], edge_send.at[side])
    for e in range(2):
        wait_bytes(scat[e].at[pl.ds(0, zs - 1)], ex_send.at[e, 0])
        wait_bytes(quad[e].at[pl.ds(0, QUAD - 1)], ex_send.at[e, 1])
        wait_bytes(full[e].at[pl.ds(0, zs - 1)], ex_send.at[e, 2])
    for step in range(2):
        wait_bytes(done.at[step, :, pl.ds(0, sps - 1)], out_send.at[step])
        wait_bytes(done.at[step, :, pl.ds(0, sps - 1)], out_recv.at[step])
        pltpu.make_async_copy(
            done.at[step, :, s], out.at[step, :, :, pl.ds(s * LANES, LANES)], own_sem.at[5 + step]
        ).wait()


def on_device(clips, sps, features, context, scene_cuts, key_clips, owner_slot):
    steps, kinds, _, frames, tokens, width = features.shape
    tiles = context.shape[1] * context.shape[2] // 8
    part = tiles // (clips // QUAD)
    zs = clips // QUAD
    key_rows = frames * sps * 8 + 2 * sps * 8 + tiles * 8
    dma = pltpu.SemaphoreType.DMA
    half = jnp.bfloat16
    smem = pl.BlockSpec(memory_space=pltpu.SMEM)
    anywhere = pl.BlockSpec(memory_space=pl.ANY)
    mixed = pl.pallas_call(
        functools.partial(kernel, clips, sps),
        out_shape=jax.ShapeDtypeStruct((steps, frames, tokens, width), half),
        in_specs=[anywhere, anywhere, smem, smem, smem],
        out_specs=anywhere,
        scratch_shapes=[
            pltpu.VMEM((steps, kinds, frames, sps, 8, LANES), half),
            pltpu.VMEM((2, 2, sps, 8, LANES), half),
            pltpu.VMEM((tiles, 8, LANES), half),
            pltpu.VMEM((zs, part, 8, LANES), half),
            pltpu.VMEM((zs, part, 8, LANES), half),
            pltpu.VMEM((2, QUAD, part, 8, LANES), half),
            pltpu.VMEM((QUAD, QUAD, part, 8, LANES), half),
            pltpu.VMEM((QUAD, QUAD, part, 8, LANES), half),
            pltpu.VMEM((zs, QUAD, part, 8, LANES), half),
            pltpu.VMEM((zs, QUAD, part, 8, LANES), half),
            pltpu.VMEM((2, key_rows, LANES), half),
            pltpu.VMEM((2, 2, key_rows, LANES), half),
            pltpu.VMEM((steps, frames, sps, 8, LANES), half),
            dma((3,)),
            dma((3,)),
            dma((7,)),
            dma((2,)),
            dma((2,)),
            dma((2, 3)),
            dma((2, 3)),
            dma((2,)),
            dma((2,)),
        ],
        compiler_params=pltpu.CompilerParams(
            collective_id=0, has_side_effects=True, vmem_limit_bytes=40 * 2**20
        ),
    )(
        features.reshape(steps, kinds, frames, tokens, width),
        context.reshape(tiles, 8, LANES),
        scene_cuts,
        key_clips,
        owner_slot.reshape(-1),
    )
    return mixed.reshape(steps, 1, frames, tokens, width)


def solution(mesh):
    placed = (
        P(None, None, "clip", None, "sp", None),
        P("clip", None, None, "sp"),
        P(),
        P(),
        P("clip", None),
    )
    return jax.shard_map(
        functools.partial(on_device, mesh.shape["clip"], mesh.shape["sp"]),
        mesh=mesh,
        in_specs=placed,
        out_specs=P(None, "clip", None, "sp", None),
        check_vma=False,
    )
```

```python
import functools

import jax
import jax.numpy as jnp
from jax import lax
from jax.experimental import pallas as pl
from jax.experimental.pallas import tpu as pltpu
from jax.sharding import PartitionSpec as P

HEAD_DIM = 64
LANES = 128
QUAD = 4
NKEY = 4
MESH = pl.DeviceIdType.MESH


def wait_bytes(ref, sem):
    pltpu.make_async_copy(ref, ref, sem).wait()


def flat(block):
    wide = block.astype(jnp.float32)
    return wide.reshape(-1, LANES).astype(jnp.bfloat16)


def kernel(
    clips,
    sps,
    feat,
    ctx,
    cuts_hbm,
    key_clips_hbm,
    slots_hbm,
    out,
    recv,
    edge,
    pooled,
    scat_0,
    scat_1,
    full_0,
    full_1,
    keys,
    vals,
    done,
    cuts,
    key_clips,
    slots,
    index_sem,
    above_sem,
    in_send,
    in_recv,
    own_sem,
    edge_send,
    edge_recv,
    ex_send,
    ex_recv,
    out_send,
    out_recv,
):
    c = lax.axis_index("clip")
    s = lax.axis_index("sp")
    zs = clips // QUAD
    z = c // QUAD
    q = c % QUAD
    frames = recv.shape[2]
    tiles = ctx.shape[0]
    part = tiles // zs
    frame_rows = sps * 8
    own_rows = frames * frame_rows
    ctx_rows = tiles * 4
    scat, full = (scat_0, scat_1), (full_0, full_1)

    small = [
        pltpu.make_async_copy(src, dst, index_sem.at[i])
        for i, (src, dst) in enumerate(((cuts_hbm, cuts), (key_clips_hbm, key_clips), (slots_hbm, slots)))
    ]
    for copy in small:
        copy.start()

    barrier = pltpu.get_barrier_semaphore()

    def greet(clip, sp):
        pl.semaphore_signal(barrier, inc=1, device_id=(clip, sp), device_id_type=MESH)

    def greet_sp(k, _):
        greet(c, (s + k) % sps)
        return 0

    def greet_quad(k, _):
        greet(z * QUAD + (q + k) % QUAD, s)
        return 0

    lax.fori_loop(1, sps, greet_sp, 0)
    lax.fori_loop(1, QUAD, greet_quad, 0)
    pl.semaphore_wait(barrier, sps - 1 + QUAD - 1 + jnp.where(z > 0, 1, 0))

    @pl.when(z < zs - 1)
    def _():
        greet(c + QUAD, s)

    def report(k, _):
        pl.semaphore_signal(above_sem, inc=1, device_id=(k * QUAD + q, s), device_id_type=MESH)
        return 0

    lax.fori_loop(0, z, report, 0)

    def remote(src, dst, send, rcv, clip, sp):
        pltpu.make_async_remote_copy(
            src_ref=src,
            dst_ref=dst,
            send_sem=send,
            recv_sem=rcv,
            device_id=(clip, sp),
            device_id_type=MESH,
        ).start()

    mid = frames // 2
    groups = (
        (0, 1, 2, 0, 1),
        (0, 1, 2, 1, frames - 1),
        (0, 0, 1, 0, frames),
        (1, 1, 2, 0, frames),
        (1, 0, 1, 0, mid),
        (1, 0, 1, mid, frames - mid),
    )

    def block(group, sp):
        step, low, size, start, count = group
        return feat.at[step, pl.ds(low, size), pl.ds(start, count), :, pl.ds(sp * LANES, LANES)]

    def place(group, sp):
        step, low, size, start, count = group
        return recv.at[step, pl.ds(low, size), pl.ds(start, count), sp]

    def others(group):
        step, low, size, start, count = group
        return recv.at[step, pl.ds(low, size), pl.ds(start, count), pl.ds(0, sps - 1)]

    def own_copy(g):
        return pltpu.make_async_copy(block(groups[g], s), place(groups[g], s), own_sem.at[g])

    def send_group(g):
        def one(k, _):
            to = (s + k) % sps
            remote(block(groups[g], to), place(groups[g], s), in_send.at[g], in_recv.at[g], c, to)
            return 0

        lax.fori_loop(1, sps, one, 0)
        own_copy(g).start()

    def wait_group(g):
        own_copy(g).wait()
        wait_bytes(others(groups[g]), in_recv.at[g])

    def scatter_own(e, src):
        return pltpu.make_async_copy(
            src.at[pl.ds(z * part, part)], scat[e].at[c], own_sem.at[len(groups) + e]
        )

    def scatter(e, src):
        def one(k, _):
            to = (c + clips - k) % clips
            remote(
                src.at[pl.ds((to // QUAD) * part, part)],
                scat[e].at[c],
                ex_send.at[e, 0],
                ex_recv.at[e, 0],
                to,
                s,
            )
            return 0

        scatter_own(e, src).start()
        lax.fori_loop(1, clips, one, 0)

    def gather(e, src):
        scatter_own(e, src).wait()
        wait_bytes(scat[e].at[pl.ds(0, clips - 1)], ex_recv.at[e, 0])
        for i in range(NKEY):
            full[e][z, i] = scat[e][key_clips[i]]

        def one(k, _):
            remote(
                full[e].at[z],
                full[e].at[z],
                ex_send.at[e, 1],
                ex_recv.at[e, 1],
                ((z + k) % zs) * QUAD + q,
                s,
            )
            return 0

        lax.fori_loop(1, zs, one, 0)

    early = z < 3 * zs // 8
    late_groups = range(3, len(groups))
    for g in range(3):
        send_group(g)

    @pl.when(early)
    def _():
        for g in late_groups:
            send_group(g)

    @pl.when(z < zs - 1)
    def _():
        pl.semaphore_wait(above_sem, zs - 1 - z)

    scatter(0, ctx)

    wait_group(0)
    half = tiles // 2
    row = lax.broadcasted_iota(jnp.int32, (half * 8, frame_rows), 0)
    col = lax.broadcasted_iota(jnp.int32, (half * 8, frame_rows), 1)
    pairs = ((col == 2 * row) | (col == 2 * row + 1)).astype(jnp.bfloat16)
    for j in range(2):
        added = jnp.dot(pairs, flat(recv[0, 1 + j, 0]), preferred_element_type=jnp.float32)
        pooled[pl.ds(j * half, half)] = (added * 2**-0.5).reshape(half, 8, LANES).astype(jnp.bfloat16)
    scatter(1, pooled)

    @pl.when(jnp.logical_not(early))
    def _():
        for g in late_groups:
            send_group(g)

    wait_group(1)

    @pl.when(c < clips - 1)
    def _():
        remote(
            recv.at[0, pl.ds(1, 2), frames - 1], edge.at[0], edge_send.at[0], edge_recv.at[0], c + 1, s
        )

    @pl.when(c > 0)
    def _():
        remote(recv.at[0, pl.ds(1, 2), 0], edge.at[1], edge_send.at[1], edge_recv.at[1], c - 1, s)

    @pl.when(c == 0)
    def _():
        edge[0] = jnp.zeros(edge.shape[1:], edge.dtype)

    @pl.when(c == clips - 1)
    def _():
        edge[1] = jnp.zeros(edge.shape[1:], edge.dtype)

    lane = lax.broadcasted_iota(jnp.int32, (1, LANES), 1)
    first = lane < HEAD_DIM

    def put(step, base, key_rows, value_rows, ok=None):
        rows = key_rows.shape[0]
        where = pl.ds(base, rows)
        ones = jnp.ones((rows, LANES), jnp.float32)
        value_rows = value_rows.astype(jnp.float32)
        if ok is not None:
            value_rows = jnp.where(ok, value_rows, 0.0)
            ones = jnp.where(ok, ones, 0.0)
        keys[step, where] = key_rows
        vals[step, 0, where] = jnp.where(first, value_rows, ones).astype(jnp.bfloat16)
        vals[step, 1, where] = jnp.where(first, ones, value_rows).astype(jnp.bfloat16)

    def put_own(step):
        for f in range(frames):
            put(step, f * frame_rows, flat(recv[step, 1, f]), flat(recv[step, 2, f]))

    def put_edge(step, before_ok, after_ok):
        for side, ok in ((0, before_ok), (1, after_ok)):
            own = recv[step, 1, 0].astype(jnp.float32)
            key_rows = jnp.where(ok, edge[side, 0].astype(jnp.float32), own)
            key_rows = key_rows.reshape(-1, LANES).astype(jnp.bfloat16)
            put(step, own_rows + side * frame_rows, key_rows, flat(edge[side, 1]), ok)

    def put_context(step):
        wait_bytes(full[step].at[pl.ds(0, zs - 1)], ex_recv.at[step, 1])
        for i in range(2):
            base = own_rows + 2 * frame_rows + i * ctx_rows
            taken = flat(full[step][:, slots[i]])
            put(step, base, taken[:ctx_rows], taken[ctx_rows:])

    def attend(step, f):
        queries = flat(recv[step, 0, f]).astype(jnp.float32) * HEAD_DIM**-0.5
        both = jnp.concatenate(
            [jnp.where(first, queries, 0.0), jnp.where(first, 0.0, queries)], axis=0
        ).astype(jnp.bfloat16)
        scores = lax.dot_general(
            both, keys[step], (((1,), (1,)), ((), ())), preferred_element_type=jnp.float32
        )
        top = jnp.max(scores, axis=1, keepdims=True)
        weights = jnp.exp(scores - top).astype(jnp.bfloat16)
        left = jnp.dot(weights[:frame_rows], vals[step, 0], preferred_element_type=jnp.float32)
        right = jnp.dot(weights[frame_rows:], vals[step, 1], preferred_element_type=jnp.float32)
        numer = jnp.where(first, left, right)
        total = pltpu.roll(jnp.where(first, right, left), HEAD_DIM, 1)
        done[step, f] = (numer / total).reshape(sps, 8, LANES).astype(jnp.bfloat16)

    parts = ((0, 0, frames), (1, 0, mid), (1, mid, frames - mid))

    def result(p, sp):
        step, start, count = parts[p]
        return done.at[step, pl.ds(start, count), sp]

    def landing(p):
        step, start, count = parts[p]
        return out.at[step, pl.ds(start, count), :, pl.ds(s * LANES, LANES)]

    def own_out(p):
        return pltpu.make_async_copy(result(p, s), landing(p), own_sem.at[len(groups) + 2 + p])

    def send_out(p):
        def one(k, _):
            to = (s + k) % sps
            remote(result(p, to), landing(p), out_send.at[p], out_recv.at[p], c, to)
            return 0

        lax.fori_loop(1, sps, one, 0)
        own_out(p).start()

    for copy in small:
        copy.wait()
    gather(0, ctx)
    put_own(0)
    gather(1, pooled)
    after = jnp.minimum(c + 1, clips - 1)
    before_ok = (c > 0) & (cuts[c] == 0)
    after_ok = (c < clips - 1) & (cuts[after] == 0)
    wait_group(2)

    @pl.when(c > 0)
    def _():
        wait_bytes(edge.at[0], edge_recv.at[0])

    @pl.when(c < clips - 1)
    def _():
        wait_bytes(edge.at[1], edge_recv.at[1])

    put_edge(0, before_ok, after_ok)
    put_context(0)
    for f in range(frames):
        attend(0, f)
    send_out(0)

    wait_group(3)
    put_own(1)
    put_edge(1, before_ok, after_ok)
    put_context(1)
    wait_group(4)
    for f in range(mid):
        attend(1, f)
    send_out(1)
    wait_group(5)
    for f in range(mid, frames):
        attend(1, f)
    send_out(2)

    for g in range(len(groups)):
        wait_bytes(others(groups[g]), in_send.at[g])

    @pl.when(c < clips - 1)
    def _():
        wait_bytes(edge.at[0], edge_send.at[0])

    @pl.when(c > 0)
    def _():
        wait_bytes(edge.at[1], edge_send.at[1])

    for e in range(2):
        wait_bytes(scat[e].at[pl.ds(0, clips - 1)], ex_send.at[e, 0])
        wait_bytes(full[e].at[pl.ds(0, zs - 1)], ex_send.at[e, 1])
    for p in range(len(parts)):
        step, start, count = parts[p]
        all_but_one = done.at[step, pl.ds(start, count), pl.ds(0, sps - 1)]
        wait_bytes(all_but_one, out_send.at[p])
        wait_bytes(all_but_one, out_recv.at[p])
        own_out(p).wait()


def on_device(clips, sps, features, context, scene_cuts, key_clips, owner_slot):
    steps, kinds, _, frames, tokens, width = features.shape
    tiles = context.shape[1] * context.shape[2] // 8
    zs = clips // QUAD
    part = tiles // zs
    key_rows = frames * sps * 8 + 2 * sps * 8 + tiles * 8
    dma = pltpu.SemaphoreType.DMA
    half = jnp.bfloat16
    anywhere = pl.BlockSpec(memory_space=pltpu.HBM)
    mixed = pl.pallas_call(
        functools.partial(kernel, clips, sps),
        out_shape=jax.ShapeDtypeStruct((steps, frames, tokens, width), half),
        in_specs=[anywhere] * 5,
        out_specs=anywhere,
        scratch_shapes=[
            pltpu.VMEM((steps, kinds, frames, sps, 8, LANES), half),
            pltpu.VMEM((2, 2, sps, 8, LANES), half),
            pltpu.VMEM((tiles, 8, LANES), half),
            pltpu.VMEM((clips, part, 8, LANES), half),
            pltpu.VMEM((clips, part, 8, LANES), half),
            pltpu.VMEM((zs, NKEY, part, 8, LANES), half),
            pltpu.VMEM((zs, NKEY, part, 8, LANES), half),
            pltpu.VMEM((2, key_rows, LANES), half),
            pltpu.VMEM((2, 2, key_rows, LANES), half),
            pltpu.VMEM((steps, frames, sps, 8, LANES), half),
            pltpu.SMEM(scene_cuts.shape, jnp.int32),
            pltpu.SMEM(key_clips.shape, jnp.int32),
            pltpu.SMEM((owner_slot.size,), jnp.int32),
            dma((3,)),
            pltpu.SemaphoreType.REGULAR,
            dma((6,)),
            dma((6,)),
            dma((11,)),
            dma((2,)),
            dma((2,)),
            dma((2, 2)),
            dma((2, 2)),
            dma((3,)),
            dma((3,)),
        ],
        compiler_params=pltpu.CompilerParams(
            collective_id=0, has_side_effects=True, vmem_limit_bytes=60 * 2**20
        ),
    )(
        features.reshape(steps, kinds, frames, tokens, width),
        context.reshape(tiles, 8, LANES),
        scene_cuts,
        key_clips,
        owner_slot.reshape(-1),
    )
    return mixed.reshape(steps, 1, frames, tokens, width)


def solution(mesh):
    placed = (
        P(None, None, "clip", None, "sp", None),
        P("clip", None, None, "sp"),
        P(),
        P(),
        P("clip", None),
    )
    return jax.shard_map(
        functools.partial(on_device, mesh.shape["clip"], mesh.shape["sp"]),
        mesh=mesh,
        in_specs=placed,
        out_specs=P(None, "clip", None, "sp", None),
        check_vma=False,
    )
```

```python
import functools

import jax
import jax.numpy as jnp
from jax import lax
from jax.experimental import pallas as pl
from jax.experimental.pallas import tpu as pltpu
from jax.sharding import PartitionSpec as P

HEAD_DIM = 64
LANES = 128
QUAD = 4
NKEY = 4
MESH = pl.DeviceIdType.MESH


def wait_bytes(ref, sem):
    pltpu.make_async_copy(ref, ref, sem).wait()


def flat(block):
    wide = block.astype(jnp.float32)
    return wide.reshape(-1, LANES).astype(jnp.bfloat16)


def kernel(
    clips,
    sps,
    feat,
    ctx,
    cuts_hbm,
    key_clips_hbm,
    slots_hbm,
    out,
    recv,
    edge,
    pooled,
    scat_0,
    scat_1,
    full_0,
    full_1,
    keys,
    vals,
    queries,
    tops,
    numers,
    totals,
    done,
    cuts,
    key_clips,
    slots,
    index_sem,
    above_sem,
    in_send,
    in_recv,
    own_sem,
    edge_send,
    edge_recv,
    ex_send,
    ex_recv,
    out_send,
    out_recv,
):
    c = lax.axis_index("clip")
    s = lax.axis_index("sp")
    zs = clips // QUAD
    z = c // QUAD
    q = c % QUAD
    frames = recv.shape[2]
    tiles = ctx.shape[0]
    part = tiles // zs
    frame_rows = sps * 8
    own_rows = frames * frame_rows
    ctx_rows = tiles * 4
    scat, full = (scat_0, scat_1), (full_0, full_1)

    small = [
        pltpu.make_async_copy(src, dst, index_sem.at[i])
        for i, (src, dst) in enumerate(((cuts_hbm, cuts), (key_clips_hbm, key_clips), (slots_hbm, slots)))
    ]
    for copy in small:
        copy.start()

    ring = sps // 2

    def partner(j, across):
        hops = ring // 2 - (j + 1) // 2
        y = (s // 2 + jnp.where(j % 2 == 1, hops, ring - hops)) % ring
        return y * 2 + (s + across) % 2

    barrier = pltpu.get_barrier_semaphore()

    def greet(clip, sp):
        pl.semaphore_signal(barrier, inc=1, device_id=(clip, sp), device_id_type=MESH)

    def greet_clip(clip, _):
        greet(clip, s)
        return 0

    def greet_quad(k, _):
        greet(z * QUAD + (q + k) % QUAD, s)
        return 0

    for across in (1, 0):

        def greet_sp(j, _):
            greet(c, partner(j, across))
            return 0

        lax.fori_loop(0, ring - 1 + across, greet_sp, 0)
    lax.fori_loop(1, QUAD, greet_quad, 0)
    lax.fori_loop((z + 1) * QUAD, clips, greet_clip, 0)
    pl.semaphore_wait(barrier, sps - 1 + QUAD - 1 + z * QUAD)

    def remote(src, dst, send, rcv, clip, sp):
        pltpu.make_async_remote_copy(
            src_ref=src,
            dst_ref=dst,
            send_sem=send,
            recv_sem=rcv,
            device_id=(clip, sp),
            device_id_type=MESH,
        ).start()

    groups = (
        (0, 1, 2, 0, 1),
        (0, 1, 2, 1, frames - 1),
        (0, 0, 1, 0, frames),
        (1, 1, 2, 0, frames),
        (1, 0, 1, 0, frames),
    )

    def block(group, sp):
        step, low, size, start, count = group
        return feat.at[step, pl.ds(low, size), pl.ds(start, count), :, pl.ds(sp * LANES, LANES)]

    def place(group, sp):
        step, low, size, start, count = group
        return recv.at[step, pl.ds(low, size), pl.ds(start, count), sp]

    def others(group):
        step, low, size, start, count = group
        return recv.at[step, pl.ds(low, size), pl.ds(start, count), pl.ds(0, sps - 1)]

    def own_copy(g):
        return pltpu.make_async_copy(block(groups[g], s), place(groups[g], s), own_sem.at[g])

    def send_group(g, across):
        def one(j, _):
            to = partner(j, across)
            remote(block(groups[g], to), place(groups[g], s), in_send.at[g], in_recv.at[g], c, to)
            return 0

        lax.fori_loop(0, ring - 1 + across, one, 0)

    def wait_group(g):
        own_copy(g).wait()
        wait_bytes(others(groups[g]), in_recv.at[g])

    def scatter_own(e, src):
        return pltpu.make_async_copy(
            src.at[pl.ds(z * part, part)], scat[e].at[c], own_sem.at[len(groups) + e]
        )

    def scatter(e, src):
        def one(j, _):
            hops = zs // 2 - (j // QUAD + 1) // 2
            plane = (z + jnp.where(j // QUAD % 2 == 1, hops, zs - hops)) % zs
            remote(
                src.at[pl.ds(plane * part, part)],
                scat[e].at[c],
                ex_send.at[e, 0],
                ex_recv.at[e, 0],
                plane * QUAD + (q + 2 + j % QUAD) % QUAD,
                s,
            )
            return 0

        def near(j, _):
            remote(
                src.at[pl.ds(z * part, part)],
                scat[e].at[c],
                ex_send.at[e, 0],
                ex_recv.at[e, 0],
                z * QUAD + (q + j) % QUAD,
                s,
            )
            return 0

        scatter_own(e, src).start()
        lax.fori_loop(0, clips - QUAD, one, 0)
        lax.fori_loop(1, QUAD, near, 0)

    def gather(e, src):
        scatter_own(e, src).wait()
        wait_bytes(scat[e].at[pl.ds(0, clips - 1)], ex_recv.at[e, 0])
        for i in range(NKEY):
            full[e][z, i] = scat[e][key_clips[i]]

        def one(k, _):
            @pl.when(k != z)
            def _():
                remote(
                    full[e].at[z],
                    full[e].at[z],
                    ex_send.at[e, 1],
                    ex_recv.at[e, 1],
                    k * QUAD + q,
                    s,
                )

            return 0

        lax.fori_loop(0, zs, one, 0)

    for across in (1, 0):
        send_group(0, across)
    for g in range(len(groups)):
        own_copy(g).start()

    def report(clip, _):
        pl.semaphore_signal(above_sem, inc=1, device_id=(clip, s), device_id_type=MESH)
        return 0

    lax.fori_loop(0, z * QUAD, report, 0)

    @pl.when(z == zs - 1)
    def _():
        scatter(0, ctx)

    early = z < zs // 2

    @pl.when(early)
    def _():
        for g in (1, 2):
            send_group(g, 1)
            send_group(g, 0)

    @pl.when(jnp.logical_not(early))
    def _():
        for g in (1, 2):
            send_group(g, 0)

    for g in (3, 4):
        send_group(g, 0)

    @pl.when(z < zs - 1)
    def _():
        pl.semaphore_wait(above_sem, (zs - 1 - z) * QUAD)
        scatter(0, ctx)
    wait_group(0)
    half = tiles // 2
    row = lax.broadcasted_iota(jnp.int32, (half * 8, frame_rows), 0)
    col = lax.broadcasted_iota(jnp.int32, (half * 8, frame_rows), 1)
    pairs = ((col == 2 * row) | (col == 2 * row + 1)).astype(jnp.bfloat16)
    for j in range(2):
        added = jnp.dot(pairs, flat(recv[0, 1 + j, 0]), preferred_element_type=jnp.float32)
        pooled[pl.ds(j * half, half)] = (added * 2**-0.5).reshape(half, 8, LANES).astype(jnp.bfloat16)
    scatter(1, pooled)

    @pl.when(jnp.logical_not(early))
    def _():
        for g in (1, 2):
            send_group(g, 1)

    for g in (3, 4):
        send_group(g, 1)

    wait_group(1)

    @pl.when(c < clips - 1)
    def _():
        remote(
            recv.at[0, pl.ds(1, 2), frames - 1], edge.at[0], edge_send.at[0], edge_recv.at[0], c + 1, s
        )

    @pl.when(c > 0)
    def _():
        remote(recv.at[0, pl.ds(1, 2), 0], edge.at[1], edge_send.at[1], edge_recv.at[1], c - 1, s)

    @pl.when(c == 0)
    def _():
        edge[0] = jnp.zeros(edge.shape[1:], edge.dtype)

    @pl.when(c == clips - 1)
    def _():
        edge[1] = jnp.zeros(edge.shape[1:], edge.dtype)

    lane = lax.broadcasted_iota(jnp.int32, (1, LANES), 1)
    first = lane < HEAD_DIM

    def put(step, base, key_rows, value_rows, ok=None):
        rows = key_rows.shape[0]
        where = pl.ds(base, rows)
        ones = jnp.ones((rows, LANES), jnp.float32)
        value_rows = value_rows.astype(jnp.float32)
        if ok is not None:
            value_rows = jnp.where(ok, value_rows, 0.0)
            ones = jnp.where(ok, ones, 0.0)
        keys[step, where] = key_rows
        vals[step, 0, where] = jnp.where(first, value_rows, ones).astype(jnp.bfloat16)
        vals[step, 1, where] = jnp.where(first, ones, value_rows).astype(jnp.bfloat16)

    def put_own(step):
        for f in range(frames):
            put(step, f * frame_rows, flat(recv[step, 1, f]), flat(recv[step, 2, f]))

    def put_edge(step, before_ok, after_ok):
        for side, ok in ((0, before_ok), (1, after_ok)):
            own = recv[step, 1, 0].astype(jnp.float32)
            key_rows = jnp.where(ok, edge[side, 0].astype(jnp.float32), own)
            key_rows = key_rows.reshape(-1, LANES).astype(jnp.bfloat16)
            put(step, own_rows + side * frame_rows, key_rows, flat(edge[side, 1]), ok)

    def put_context(step):
        wait_bytes(full[step].at[pl.ds(0, zs - 1)], ex_recv.at[step, 1])
        for i in range(2):
            base = own_rows + 2 * frame_rows + i * ctx_rows
            taken = flat(full[step][:, slots[i]])
            put(step, base, taken[:ctx_rows], taken[ctx_rows:])

    context_start = own_rows + 2 * frame_rows

    def weigh(step, f, low, count, top):
        scores = lax.dot_general(
            queries[step, f],
            keys[step, pl.ds(low, count)],
            (((1,), (1,)), ((), ())),
            preferred_element_type=jnp.float32,
        )
        high = jnp.max(scores, axis=1, keepdims=True)
        if top is not None:
            high = jnp.maximum(high, top)
        weights = jnp.exp(scores - high).astype(jnp.bfloat16)
        where = pl.ds(low, count)
        left = jnp.dot(weights[:frame_rows], vals[step, 0, where], preferred_element_type=jnp.float32)
        right = jnp.dot(weights[frame_rows:], vals[step, 1, where], preferred_element_type=jnp.float32)
        return high, jnp.where(first, left, right), jnp.where(first, right, left)

    def attend_near(step, f):
        rows = flat(recv[step, 0, f]).astype(jnp.float32) * HEAD_DIM**-0.5
        queries[step, f] = jnp.concatenate(
            [jnp.where(first, rows, 0.0), jnp.where(first, 0.0, rows)], axis=0
        ).astype(jnp.bfloat16)
        high, numer, total = weigh(step, f, 0, context_start, None)
        tops[step, f] = jnp.broadcast_to(high, (2 * frame_rows, LANES))
        numers[step, f] = numer
        totals[step, f] = total

    def attend_context(step, f):
        top = tops[step, f]
        high, numer, total = weigh(step, f, context_start, 2 * ctx_rows, top[:, :1])
        scale = jnp.exp(top - high)
        left, right = scale[:frame_rows], scale[frame_rows:]
        numer = numer + numers[step, f] * jnp.where(first, left, right)
        total = total + totals[step, f] * jnp.where(first, right, left)
        total = pltpu.roll(total, HEAD_DIM, 1)
        done[step, f] = (numer / total).reshape(sps, 8, LANES).astype(jnp.bfloat16)

    parts = ((0, 0, frames), (1, 0, frames))

    def result(p, sp):
        step, start, count = parts[p]
        return done.at[step, pl.ds(start, count), sp]

    def landing(p):
        step, start, count = parts[p]
        return out.at[step, pl.ds(start, count), :, pl.ds(s * LANES, LANES)]

    def own_out(p):
        return pltpu.make_async_copy(result(p, s), landing(p), own_sem.at[len(groups) + 2 + p])

    def send_out(p):
        for across in (1, 0):

            def one(j, _):
                to = partner(j, across)
                remote(result(p, to), landing(p), out_send.at[p], out_recv.at[p], c, to)
                return 0

            lax.fori_loop(0, ring - 1 + across, one, 0)
        own_out(p).start()

    for copy in small:
        copy.wait()
    gather(0, ctx)
    gather(1, pooled)
    after = jnp.minimum(c + 1, clips - 1)
    before_ok = (c > 0) & (cuts[c] == 0)
    after_ok = (c < clips - 1) & (cuts[after] == 0)

    @pl.when(c > 0)
    def _():
        wait_bytes(edge.at[0], edge_recv.at[0])

    @pl.when(c < clips - 1)
    def _():
        wait_bytes(edge.at[1], edge_recv.at[1])

    for step in range(2):
        for g in range(1 + 2 * step, 3 + 2 * step):
            if g != 1:
                wait_group(g)
        put_own(step)
        put_edge(step, before_ok, after_ok)
        for f in range(frames):
            attend_near(step, f)
    for step in range(2):
        put_context(step)
        for f in range(frames):
            attend_context(step, f)
        send_out(step)

    for g in range(len(groups)):
        wait_bytes(others(groups[g]), in_send.at[g])

    @pl.when(c < clips - 1)
    def _():
        wait_bytes(edge.at[0], edge_send.at[0])

    @pl.when(c > 0)
    def _():
        wait_bytes(edge.at[1], edge_send.at[1])

    for e in range(2):
        wait_bytes(scat[e].at[pl.ds(0, clips - 1)], ex_send.at[e, 0])
        wait_bytes(full[e].at[pl.ds(0, zs - 1)], ex_send.at[e, 1])
    for p in range(len(parts)):
        step, start, count = parts[p]
        all_but_one = done.at[step, pl.ds(start, count), pl.ds(0, sps - 1)]
        wait_bytes(all_but_one, out_send.at[p])
        wait_bytes(all_but_one, out_recv.at[p])
        own_out(p).wait()


def on_device(clips, sps, features, context, scene_cuts, key_clips, owner_slot):
    steps, kinds, _, frames, tokens, width = features.shape
    tiles = context.shape[1] * context.shape[2] // 8
    zs = clips // QUAD
    part = tiles // zs
    frame_rows = sps * 8
    key_rows = (frames + 2) * frame_rows + tiles * 8
    dma = pltpu.SemaphoreType.DMA
    half = jnp.bfloat16
    anywhere = pl.BlockSpec(memory_space=pltpu.HBM)
    mixed = pl.pallas_call(
        functools.partial(kernel, clips, sps),
        out_shape=pltpu.VMEM((steps, frames, tokens, width), half),
        in_specs=[anywhere] * 5,
        out_specs=pl.BlockSpec(memory_space=pltpu.VMEM),
        scratch_shapes=[
            pltpu.VMEM((steps, kinds, frames, sps, 8, LANES), half),
            pltpu.VMEM((2, 2, sps, 8, LANES), half),
            pltpu.VMEM((tiles, 8, LANES), half),
            pltpu.VMEM((clips, part, 8, LANES), half),
            pltpu.VMEM((clips, part, 8, LANES), half),
            pltpu.VMEM((zs, NKEY, part, 8, LANES), half),
            pltpu.VMEM((zs, NKEY, part, 8, LANES), half),
            pltpu.VMEM((2, key_rows, LANES), half),
            pltpu.VMEM((2, 2, key_rows, LANES), half),
            pltpu.VMEM((steps, frames, 2 * frame_rows, LANES), half),
            pltpu.VMEM((steps, frames, 2 * frame_rows, LANES), jnp.float32),
            pltpu.VMEM((steps, frames, frame_rows, LANES), jnp.float32),
            pltpu.VMEM((steps, frames, frame_rows, LANES), jnp.float32),
            pltpu.VMEM((steps, frames, sps, 8, LANES), half),
            pltpu.SMEM(scene_cuts.shape, jnp.int32),
            pltpu.SMEM(key_clips.shape, jnp.int32),
            pltpu.SMEM((owner_slot.size,), jnp.int32),
            dma((3,)),
            pltpu.SemaphoreType.REGULAR,
            dma((5,)),
            dma((5,)),
            dma((9,)),
            dma((2,)),
            dma((2,)),
            dma((2, 2)),
            dma((2, 2)),
            dma((2,)),
            dma((2,)),
        ],
        compiler_params=pltpu.CompilerParams(
            collective_id=0, has_side_effects=True, vmem_limit_bytes=60 * 2**20
        ),
    )(
        features.reshape(steps, kinds, frames, tokens, width),
        context.reshape(tiles, 8, LANES),
        scene_cuts,
        key_clips,
        owner_slot.reshape(-1),
    )
    return mixed.reshape(steps, 1, frames, tokens, width)


def solution(mesh):
    placed = (
        P(None, None, "clip", None, "sp", None),
        P("clip", None, None, "sp"),
        P(),
        P(),
        P("clip", None),
    )
    return jax.shard_map(
        functools.partial(on_device, mesh.shape["clip"], mesh.shape["sp"]),
        mesh=mesh,
        in_specs=placed,
        out_specs=P(None, "clip", None, "sp", None),
        check_vma=False,
    )
```

```python
import functools

import jax
import jax.numpy as jnp
from jax import lax
from jax.experimental import pallas as pl
from jax.experimental.pallas import tpu as pltpu
from jax.sharding import PartitionSpec as P

HEAD_DIM = 64
LANES = 128
QUAD = 4
NKEY = 4
MESH = pl.DeviceIdType.MESH


def wait_bytes(ref, sem):
    pltpu.make_async_copy(ref, ref, sem).wait()


def flat(block):
    wide = block.astype(jnp.float32)
    return wide.reshape(-1, LANES).astype(jnp.bfloat16)


def kernel(
    clips,
    sps,
    feat,
    ctx,
    cuts_hbm,
    key_clips_hbm,
    slots_hbm,
    out,
    recv,
    edge,
    pooled,
    scat_0,
    scat_1,
    full_0,
    full_1,
    keys,
    vals,
    queries,
    tops,
    numers,
    totals,
    done,
    cuts,
    key_clips,
    slots,
    index_sem,
    above_sem,
    in_send,
    in_recv,
    own_sem,
    edge_send,
    edge_recv,
    ex_send,
    ex_recv,
    out_send,
    out_recv,
):
    c = lax.axis_index("clip")
    s = lax.axis_index("sp")
    zs = clips // QUAD
    z = c // QUAD
    q = c % QUAD
    frames = recv.shape[2]
    tiles = ctx.shape[0]
    part = tiles // zs
    frame_rows = sps * 8
    own_rows = frames * frame_rows
    ctx_rows = tiles * 4
    scat, full = (scat_0, scat_1), (full_0, full_1)

    small = [
        pltpu.make_async_copy(src, dst, index_sem.at[i])
        for i, (src, dst) in enumerate(((cuts_hbm, cuts), (key_clips_hbm, key_clips), (slots_hbm, slots)))
    ]
    for copy in small:
        copy.start()

    ring = sps // 2

    def partner(j, across):
        hops = ring // 2 - (j + 1) // 2
        y = (s // 2 + jnp.where(j % 2 == 1, hops, ring - hops)) % ring
        return y * 2 + (s + across) % 2

    barrier = pltpu.get_barrier_semaphore()

    def greet(clip, sp):
        pl.semaphore_signal(barrier, inc=1, device_id=(clip, sp), device_id_type=MESH)

    def greet_clip(clip, _):
        greet(clip, s)
        return 0

    def greet_quad(k, _):
        greet(z * QUAD + (q + k) % QUAD, s)
        return 0

    for across in (1, 0):

        def greet_sp(j, _):
            greet(c, partner(j, across))
            return 0

        lax.fori_loop(0, ring - 1 + across, greet_sp, 0)
    lax.fori_loop(1, QUAD, greet_quad, 0)
    lax.fori_loop((z + 1) * QUAD, clips, greet_clip, 0)
    pl.semaphore_wait(barrier, sps - 1 + QUAD - 1 + z * QUAD)

    def remote(src, dst, send, rcv, clip, sp):
        pltpu.make_async_remote_copy(
            src_ref=src,
            dst_ref=dst,
            send_sem=send,
            recv_sem=rcv,
            device_id=(clip, sp),
            device_id_type=MESH,
        ).start()

    groups = (
        (0, 1, 2, 0, 1),
        (0, 1, 2, 1, frames - 1),
        (0, 0, 1, 0, frames),
        (1, 1, 2, 0, frames),
        (1, 0, 1, 0, frames),
    )

    def block(group, sp):
        step, low, size, start, count = group
        return feat.at[step, pl.ds(low, size), pl.ds(start, count), :, pl.ds(sp * LANES, LANES)]

    def place(group, sp):
        step, low, size, start, count = group
        return recv.at[step, pl.ds(low, size), pl.ds(start, count), sp]

    def others(group):
        step, low, size, start, count = group
        return recv.at[step, pl.ds(low, size), pl.ds(start, count), pl.ds(0, sps - 1)]

    def own_copy(g):
        return pltpu.make_async_copy(block(groups[g], s), place(groups[g], s), own_sem.at[g])

    def send_group(g, across):
        def one(j, _):
            to = partner(j, across)
            remote(block(groups[g], to), place(groups[g], s), in_send.at[g], in_recv.at[g], c, to)
            return 0

        lax.fori_loop(0, ring - 1 + across, one, 0)

    def wait_group(g):
        own_copy(g).wait()
        wait_bytes(others(groups[g]), in_recv.at[g])

    def scatter_own(e, src):
        return pltpu.make_async_copy(
            src.at[pl.ds(z * part, part)], scat[e].at[c], own_sem.at[len(groups) + e]
        )

    def scatter(e, src):
        def one(j, _):
            hops = zs // 2 - (j // QUAD + 1) // 2
            plane = (z + jnp.where(j // QUAD % 2 == 1, hops, zs - hops)) % zs
            remote(
                src.at[pl.ds(plane * part, part)],
                scat[e].at[c],
                ex_send.at[e, 0],
                ex_recv.at[e, 0],
                plane * QUAD + (q + 2 + j % QUAD) % QUAD,
                s,
            )
            return 0

        def near(j, _):
            remote(
                src.at[pl.ds(z * part, part)],
                scat[e].at[c],
                ex_send.at[e, 0],
                ex_recv.at[e, 0],
                z * QUAD + (q + j) % QUAD,
                s,
            )
            return 0

        scatter_own(e, src).start()
        lax.fori_loop(0, clips - QUAD, one, 0)
        lax.fori_loop(1, QUAD, near, 0)

    def gather(e, src):
        scatter_own(e, src).wait()
        wait_bytes(scat[e].at[pl.ds(0, clips - 1)], ex_recv.at[e, 0])
        for i in range(NKEY):
            full[e][z, i] = scat[e][key_clips[i]]

        def one(k, _):
            @pl.when(k != z)
            def _():
                remote(
                    full[e].at[z],
                    full[e].at[z],
                    ex_send.at[e, 1],
                    ex_recv.at[e, 1],
                    k * QUAD + q,
                    s,
                )

            return 0

        lax.fori_loop(0, zs, one, 0)

    for across in (1, 0):
        send_group(0, across)
    for g in range(len(groups)):
        own_copy(g).start()

    def report(clip, _):
        pl.semaphore_signal(above_sem, inc=1, device_id=(clip, s), device_id_type=MESH)
        return 0

    lax.fori_loop(0, z * QUAD, report, 0)

    @pl.when(z == zs - 1)
    def _():
        scatter(0, ctx)

    early = z < zs // 2
    hold = z >= 3 * zs // 4

    @pl.when(jnp.logical_not(hold))
    def _():
        for g in (1, 2):
            send_group(g, 1)
            send_group(g, 0)

    @pl.when(hold)
    def _():
        for g in (1, 2):
            send_group(g, 0)

    for g in (3, 4):
        send_group(g, 0)

    @pl.when(z < 2)
    def _():
        for g in (3, 4):
            send_group(g, 1)

    @pl.when(z < zs - 1)
    def _():
        pl.semaphore_wait(above_sem, (zs - 1 - z) * QUAD)
        scatter(0, ctx)
    wait_group(0)
    half = tiles // 2
    row = lax.broadcasted_iota(jnp.int32, (half * 8, frame_rows), 0)
    col = lax.broadcasted_iota(jnp.int32, (half * 8, frame_rows), 1)
    pairs = ((col == 2 * row) | (col == 2 * row + 1)).astype(jnp.bfloat16)
    for j in range(2):
        added = jnp.dot(pairs, flat(recv[0, 1 + j, 0]), preferred_element_type=jnp.float32)
        pooled[pl.ds(j * half, half)] = (added * 2**-0.5).reshape(half, 8, LANES).astype(jnp.bfloat16)
    scatter(1, pooled)

    @pl.when(hold)
    def _():
        for g in (1, 2):
            send_group(g, 1)

    @pl.when(z >= 2)
    def _():
        for g in (3, 4):
            send_group(g, 1)

    lane = lax.broadcasted_iota(jnp.int32, (1, LANES), 1)
    first = lane < HEAD_DIM

    def put(step, base, key_rows, value_rows, ok=None):
        rows = key_rows.shape[0]
        where = pl.ds(base, rows)
        ones = jnp.ones((rows, LANES), jnp.float32)
        value_rows = value_rows.astype(jnp.float32)
        if ok is not None:
            value_rows = jnp.where(ok, value_rows, 0.0)
            ones = jnp.where(ok, ones, 0.0)
        keys[step, where] = key_rows
        vals[step, 0, where] = jnp.where(first, value_rows, ones).astype(jnp.bfloat16)
        vals[step, 1, where] = jnp.where(first, ones, value_rows).astype(jnp.bfloat16)

    def put_own(step):
        for f in range(frames):
            put(step, f * frame_rows, flat(recv[step, 1, f]), flat(recv[step, 2, f]))

    def put_edge(step, before_ok, after_ok):
        for side, ok in ((0, before_ok), (1, after_ok)):
            own = recv[step, 1, 0].astype(jnp.float32)
            key_rows = jnp.where(ok, edge[side, 0].astype(jnp.float32), own)
            key_rows = key_rows.reshape(-1, LANES).astype(jnp.bfloat16)
            put(step, own_rows + side * frame_rows, key_rows, flat(edge[side, 1]), ok)

    def put_context(step):
        wait_bytes(full[step].at[pl.ds(0, zs - 1)], ex_recv.at[step, 1])
        for i in range(2):
            base = own_rows + 2 * frame_rows + i * ctx_rows
            taken = flat(full[step][:, slots[i]])
            put(step, base, taken[:ctx_rows], taken[ctx_rows:])

    context_start = own_rows + 2 * frame_rows

    def weigh(step, f, low, count, top):
        scores = lax.dot_general(
            queries[step, f],
            keys[step, pl.ds(low, count)],
            (((1,), (1,)), ((), ())),
            preferred_element_type=jnp.float32,
        )
        high = jnp.max(scores, axis=1, keepdims=True)
        if top is not None:
            high = jnp.maximum(high, top)
        weights = jnp.exp(scores - high).astype(jnp.bfloat16)
        where = pl.ds(low, count)
        left = jnp.dot(weights[:frame_rows], vals[step, 0, where], preferred_element_type=jnp.float32)
        right = jnp.dot(weights[frame_rows:], vals[step, 1, where], preferred_element_type=jnp.float32)
        return high, jnp.where(first, left, right), jnp.where(first, right, left)

    def attend_near(step, f):
        rows = flat(recv[step, 0, f]).astype(jnp.float32) * HEAD_DIM**-0.5
        queries[step, f] = jnp.concatenate(
            [jnp.where(first, rows, 0.0), jnp.where(first, 0.0, rows)], axis=0
        ).astype(jnp.bfloat16)
        high, numer, total = weigh(step, f, 0, context_start, None)
        tops[step, f] = jnp.broadcast_to(high, (2 * frame_rows, LANES))
        numers[step, f] = numer
        totals[step, f] = total

    def attend_context(step, f):
        top = tops[step, f]
        high, numer, total = weigh(step, f, context_start, 2 * ctx_rows, top[:, :1])
        scale = jnp.exp(top - high)
        left, right = scale[:frame_rows], scale[frame_rows:]
        numer = numer + numers[step, f] * jnp.where(first, left, right)
        total = total + totals[step, f] * jnp.where(first, right, left)
        total = pltpu.roll(total, HEAD_DIM, 1)
        done[step, f] = (numer / total).reshape(sps, 8, LANES).astype(jnp.bfloat16)

    parts = ((0, 0, frames), (1, 0, frames))

    def result(p, sp):
        step, start, count = parts[p]
        return done.at[step, pl.ds(start, count), sp]

    def landing(p):
        step, start, count = parts[p]
        return out.at[step, pl.ds(start, count), :, pl.ds(s * LANES, LANES)]

    def own_out(p):
        return pltpu.make_async_copy(result(p, s), landing(p), own_sem.at[len(groups) + 2 + p])

    def send_out(p):
        for across in (1, 0):

            def one(j, _):
                to = partner(j, across)
                remote(result(p, to), landing(p), out_send.at[p], out_recv.at[p], c, to)
                return 0

            lax.fori_loop(0, ring - 1 + across, one, 0)
        own_out(p).start()

    def send_edges():
        wait_group(1)

        @pl.when(c < clips - 1)
        def _():
            remote(
                recv.at[0, pl.ds(1, 2), frames - 1], edge.at[0], edge_send.at[0], edge_recv.at[0], c + 1, s
            )

        @pl.when(c > 0)
        def _():
            remote(recv.at[0, pl.ds(1, 2), 0], edge.at[1], edge_send.at[1], edge_recv.at[1], c - 1, s)

        @pl.when(c == 0)
        def _():
            edge[0] = jnp.zeros(edge.shape[1:], edge.dtype)

        @pl.when(c == clips - 1)
        def _():
            edge[1] = jnp.zeros(edge.shape[1:], edge.dtype)

    def collect():
        gather(0, ctx)
        gather(1, pooled)

    for copy in small:
        copy.wait()

    after = jnp.minimum(c + 1, clips - 1)
    before_ok = (c > 0) & (cuts[c] == 0)
    after_ok = (c < clips - 1) & (cuts[after] == 0)

    def near(step):
        if step == 1:
            wait_group(3)
        put_own(step)
        put_edge(step, before_ok, after_ok)
        wait_group(2 + 2 * step)
        for f in range(frames):
            attend_near(step, f)

    def finish(step):
        put_context(step)
        for f in range(frames):
            attend_context(step, f)
        send_out(step)

    def wait_edges():
        @pl.when(c > 0)
        def _():
            wait_bytes(edge.at[0], edge_recv.at[0])

        @pl.when(c < clips - 1)
        def _():
            wait_bytes(edge.at[1], edge_recv.at[1])

    first_planes = z < zs // 4

    @pl.when(first_planes)
    def _():
        send_edges()
        wait_edges()
        near(0)
        collect()

    @pl.when(jnp.logical_not(first_planes | hold))
    def _():
        send_edges()

    @pl.when(jnp.logical_not(first_planes))
    def _():
        collect()

    @pl.when(hold)
    def _():
        send_edges()

    @pl.when(jnp.logical_not(first_planes))
    def _():
        wait_edges()
        near(0)

    finish(0)
    near(1)
    finish(1)

    for g in range(len(groups)):
        wait_bytes(others(groups[g]), in_send.at[g])

    @pl.when(c < clips - 1)
    def _():
        wait_bytes(edge.at[0], edge_send.at[0])

    @pl.when(c > 0)
    def _():
        wait_bytes(edge.at[1], edge_send.at[1])

    for e in range(2):
        wait_bytes(scat[e].at[pl.ds(0, clips - 1)], ex_send.at[e, 0])
        wait_bytes(full[e].at[pl.ds(0, zs - 1)], ex_send.at[e, 1])
    for p in range(len(parts)):
        step, start, count = parts[p]
        all_but_one = done.at[step, pl.ds(start, count), pl.ds(0, sps - 1)]
        wait_bytes(all_but_one, out_send.at[p])
        wait_bytes(all_but_one, out_recv.at[p])
        own_out(p).wait()


def on_device(clips, sps, features, context, scene_cuts, key_clips, owner_slot):
    steps, kinds, _, frames, tokens, width = features.shape
    tiles = context.shape[1] * context.shape[2] // 8
    zs = clips // QUAD
    part = tiles // zs
    frame_rows = sps * 8
    key_rows = (frames + 2) * frame_rows + tiles * 8
    dma = pltpu.SemaphoreType.DMA
    half = jnp.bfloat16
    anywhere = pl.BlockSpec(memory_space=pltpu.HBM)
    mixed = pl.pallas_call(
        functools.partial(kernel, clips, sps),
        out_shape=pltpu.VMEM((steps, frames, tokens, width), half),
        in_specs=[anywhere] * 5,
        out_specs=pl.BlockSpec(memory_space=pltpu.VMEM),
        scratch_shapes=[
            pltpu.VMEM((steps, kinds, frames, sps, 8, LANES), half),
            pltpu.VMEM((2, 2, sps, 8, LANES), half),
            pltpu.VMEM((tiles, 8, LANES), half),
            pltpu.VMEM((clips, part, 8, LANES), half),
            pltpu.VMEM((clips, part, 8, LANES), half),
            pltpu.VMEM((zs, NKEY, part, 8, LANES), half),
            pltpu.VMEM((zs, NKEY, part, 8, LANES), half),
            pltpu.VMEM((2, key_rows, LANES), half),
            pltpu.VMEM((2, 2, key_rows, LANES), half),
            pltpu.VMEM((steps, frames, 2 * frame_rows, LANES), half),
            pltpu.VMEM((steps, frames, 2 * frame_rows, LANES), jnp.float32),
            pltpu.VMEM((steps, frames, frame_rows, LANES), jnp.float32),
            pltpu.VMEM((steps, frames, frame_rows, LANES), jnp.float32),
            pltpu.VMEM((steps, frames, sps, 8, LANES), half),
            pltpu.SMEM(scene_cuts.shape, jnp.int32),
            pltpu.SMEM(key_clips.shape, jnp.int32),
            pltpu.SMEM((owner_slot.size,), jnp.int32),
            dma((3,)),
            pltpu.SemaphoreType.REGULAR,
            dma((5,)),
            dma((5,)),
            dma((9,)),
            dma((2,)),
            dma((2,)),
            dma((2, 2)),
            dma((2, 2)),
            dma((2,)),
            dma((2,)),
        ],
        compiler_params=pltpu.CompilerParams(
            collective_id=0, has_side_effects=True, vmem_limit_bytes=60 * 2**20
        ),
    )(
        features.reshape(steps, kinds, frames, tokens, width),
        context.reshape(tiles, 8, LANES),
        scene_cuts,
        key_clips,
        owner_slot.reshape(-1),
    )
    return mixed.reshape(steps, 1, frames, tokens, width)


def solution(mesh):
    placed = (
        P(None, None, "clip", None, "sp", None),
        P("clip", None, None, "sp"),
        P(),
        P(),
        P("clip", None),
    )
    return jax.shard_map(
        functools.partial(on_device, mesh.shape["clip"], mesh.shape["sp"]),
        mesh=mesh,
        in_specs=placed,
        out_specs=P(None, "clip", None, "sp", None),
        check_vma=False,
    )
```

```python
import functools

import jax
import jax.numpy as jnp
from jax import lax
from jax.experimental import pallas as pl
from jax.experimental.pallas import tpu as pltpu
from jax.sharding import PartitionSpec as P

HEAD_DIM = 64
LANES = 128
QUAD = 4
NKEY = 4
MESH = pl.DeviceIdType.MESH


def wait_bytes(ref, sem):
    pltpu.make_async_copy(ref, ref, sem).wait()


def flat(block):
    wide = block.astype(jnp.float32)
    return wide.reshape(-1, LANES).astype(jnp.bfloat16)


def kernel(
    clips,
    sps,
    feat,
    ctx,
    cuts_hbm,
    key_clips_hbm,
    slots_hbm,
    out,
    recv,
    edge,
    pooled,
    scat_0,
    scat_1,
    full_0,
    full_1,
    keys,
    vals,
    queries,
    tops,
    numers,
    totals,
    done,
    cuts,
    key_clips,
    slots,
    index_sem,
    above_sem,
    in_send,
    in_recv,
    own_sem,
    edge_send,
    edge_recv,
    ex_send,
    ex_recv,
    out_send,
    out_recv,
):
    c = lax.axis_index("clip")
    s = lax.axis_index("sp")
    zs = clips // QUAD
    z = c // QUAD
    q = c % QUAD
    frames = recv.shape[2]
    tiles = ctx.shape[0]
    part = tiles // zs
    frame_rows = sps * 8
    own_rows = frames * frame_rows
    ctx_rows = tiles * 4
    scat, full = (scat_0, scat_1), (full_0, full_1)

    small = [
        pltpu.make_async_copy(src, dst, index_sem.at[i])
        for i, (src, dst) in enumerate(((cuts_hbm, cuts), (key_clips_hbm, key_clips), (slots_hbm, slots)))
    ]

    ring = sps // 2

    def partner(j, across):
        hops = ring // 2 - (j + 1) // 2
        y = (s // 2 + jnp.where(j % 2 == 1, hops, ring - hops)) % ring
        return y * 2 + (s + across) % 2

    barrier = pltpu.get_barrier_semaphore()

    def greet(clip, sp):
        pl.semaphore_signal(barrier, inc=1, device_id=(clip, sp), device_id_type=MESH)

    def greet_clip(clip, _):
        greet(clip, s)
        return 0

    def greet_quad(k, _):
        greet(z * QUAD + (q + k) % QUAD, s)
        return 0

    for across in (1, 0):

        def greet_sp(j, _):
            greet(c, partner(j, across))
            return 0

        lax.fori_loop(0, ring - 1 + across, greet_sp, 0)
    lax.fori_loop(1, QUAD, greet_quad, 0)
    lax.fori_loop((z + 1) * QUAD, clips, greet_clip, 0)
    for copy in small:
        copy.start()
    pl.semaphore_wait(barrier, sps - 1 + QUAD - 1 + z * QUAD)

    def remote(src, dst, send, rcv, clip, sp):
        pltpu.make_async_remote_copy(
            src_ref=src,
            dst_ref=dst,
            send_sem=send,
            recv_sem=rcv,
            device_id=(clip, sp),
            device_id_type=MESH,
        ).start()

    groups = (
        (0, 1, 2, 0, 1),
        (0, 1, 2, 1, frames - 1),
        (0, 0, 1, 0, frames),
        (1, 1, 2, 0, frames),
        (1, 0, 1, 0, frames),
    )

    def block(group, sp):
        step, low, size, start, count = group
        return feat.at[step, pl.ds(low, size), pl.ds(start, count), :, pl.ds(sp * LANES, LANES)]

    def place(group, sp):
        step, low, size, start, count = group
        return recv.at[step, pl.ds(low, size), pl.ds(start, count), sp]

    def others(group):
        step, low, size, start, count = group
        return recv.at[step, pl.ds(low, size), pl.ds(start, count), pl.ds(0, sps - 1)]

    def own_copy(g):
        return pltpu.make_async_copy(block(groups[g], s), place(groups[g], s), own_sem.at[g])

    def send_group(g, across):
        def one(j, _):
            to = partner(j, across)
            remote(block(groups[g], to), place(groups[g], s), in_send.at[g], in_recv.at[g], c, to)
            return 0

        lax.fori_loop(0, ring - 1 + across, one, 0)

    def wait_group(g):
        own_copy(g).wait()
        wait_bytes(others(groups[g]), in_recv.at[g])

    def scatter_own(e, src):
        return pltpu.make_async_copy(
            src.at[pl.ds(z * part, part)], scat[e].at[c], own_sem.at[len(groups) + e]
        )

    def scatter(e, src):
        def one(j, _):
            plane = (z + 1 + j // QUAD) % zs
            remote(
                src.at[pl.ds(plane * part, part)],
                scat[e].at[c],
                ex_send.at[e, 0],
                ex_recv.at[e, 0],
                plane * QUAD + (q + 2 + j % QUAD) % QUAD,
                s,
            )
            return 0

        def near(j, _):
            remote(
                src.at[pl.ds(z * part, part)],
                scat[e].at[c],
                ex_send.at[e, 0],
                ex_recv.at[e, 0],
                z * QUAD + (q + j) % QUAD,
                s,
            )
            return 0

        scatter_own(e, src).start()
        lax.fori_loop(0, clips - QUAD, one, 0)
        lax.fori_loop(1, QUAD, near, 0)

    def gather(e, src):
        scatter_own(e, src).wait()
        wait_bytes(scat[e].at[pl.ds(0, clips - 1)], ex_recv.at[e, 0])
        for i in range(NKEY):
            full[e][z, i] = scat[e][key_clips[i]]

        def one(k, _):
            @pl.when(k != z)
            def _():
                remote(
                    full[e].at[z],
                    full[e].at[z],
                    ex_send.at[e, 1],
                    ex_recv.at[e, 1],
                    k * QUAD + q,
                    s,
                )

            return 0

        lax.fori_loop(0, zs, one, 0)

    for across in (1, 0):
        send_group(0, across)
    for g in range(len(groups)):
        own_copy(g).start()

    def report(clip, _):
        pl.semaphore_signal(above_sem, inc=1, device_id=(clip, s), device_id_type=MESH)
        return 0

    lax.fori_loop(0, z * QUAD, report, 0)

    @pl.when(z == zs - 1)
    def _():
        scatter(0, ctx)

    early = z < zs // 2
    hold = z >= 3 * zs // 4

    @pl.when(jnp.logical_not(hold))
    def _():
        for g in (1, 2):
            send_group(g, 1)
            send_group(g, 0)

    @pl.when(hold)
    def _():
        for g in (1, 2):
            send_group(g, 0)

    for g in (3, 4):
        send_group(g, 0)

    @pl.when(z < 2)
    def _():
        for g in (3, 4):
            send_group(g, 1)

    @pl.when(z < zs - 1)
    def _():
        pl.semaphore_wait(above_sem, (zs - 1 - z) * QUAD)
        scatter(0, ctx)
    wait_group(0)
    half = tiles // 2
    row = lax.broadcasted_iota(jnp.int32, (half * 8, frame_rows), 0)
    col = lax.broadcasted_iota(jnp.int32, (half * 8, frame_rows), 1)
    pairs = ((col == 2 * row) | (col == 2 * row + 1)).astype(jnp.bfloat16)
    for j in range(2):
        added = jnp.dot(pairs, flat(recv[0, 1 + j, 0]), preferred_element_type=jnp.float32)
        pooled[pl.ds(j * half, half)] = (added * 2**-0.5).reshape(half, 8, LANES).astype(jnp.bfloat16)
    scatter(1, pooled)

    @pl.when(hold)
    def _():
        for g in (1, 2):
            send_group(g, 1)

    @pl.when(z >= 2)
    def _():
        for g in (3, 4):
            send_group(g, 1)

    lane = lax.broadcasted_iota(jnp.int32, (1, LANES), 1)
    first = lane < HEAD_DIM

    def put(step, base, key_rows, value_rows, ok=None):
        rows = key_rows.shape[0]
        where = pl.ds(base, rows)
        ones = jnp.ones((rows, LANES), jnp.bfloat16)
        if ok is not None:
            value_rows = jnp.where(ok, value_rows, jnp.zeros_like(value_rows))
            ones = jnp.where(ok, ones, jnp.zeros_like(ones))
        keys[step, where] = key_rows
        vals[step, 0, where] = jnp.where(first, value_rows, ones)
        vals[step, 1, where] = jnp.where(first, ones, value_rows)

    def put_own(step):
        for f in range(frames):
            put(step, f * frame_rows, flat(recv[step, 1, f]), flat(recv[step, 2, f]))

    def put_edge(step, before_ok, after_ok):
        for side, ok in ((0, before_ok), (1, after_ok)):
            own = recv[step, 1, 0].astype(jnp.float32)
            key_rows = jnp.where(ok, edge[side, 0].astype(jnp.float32), own)
            key_rows = key_rows.reshape(-1, LANES).astype(jnp.bfloat16)
            put(step, own_rows + side * frame_rows, key_rows, flat(edge[side, 1]), ok)

    def put_context(step):
        wait_bytes(full[step].at[pl.ds(0, zs - 1)], ex_recv.at[step, 1])
        for i in range(2):
            base = own_rows + 2 * frame_rows + i * ctx_rows
            taken = flat(full[step][:, slots[i]])
            put(step, base, taken[:ctx_rows], taken[ctx_rows:])

    context_start = own_rows + 2 * frame_rows

    def weigh(step, f, low, count, top):
        scores = lax.dot_general(
            queries[step, f],
            keys[step, pl.ds(low, count)],
            (((1,), (1,)), ((), ())),
            preferred_element_type=jnp.float32,
        )
        high = jnp.max(scores, axis=1, keepdims=True)
        if top is not None:
            high = jnp.maximum(high, top)
        weights = jnp.exp(scores - high).astype(jnp.bfloat16)
        where = pl.ds(low, count)
        left = jnp.dot(weights[:block_rows], vals[step, 0, where], preferred_element_type=jnp.float32)
        right = jnp.dot(weights[block_rows:], vals[step, 1, where], preferred_element_type=jnp.float32)
        return high, jnp.where(first, left, right), jnp.where(first, right, left)

    columns = max(ring // 4, 1)
    blocks = ring // columns
    part_rows = 2 * frames * 8
    block_rows = columns * part_rows

    def origins(f):
        for j in range(f * columns, (f + 1) * columns):
            hops = ring // 2 - (j + 1) // 2
            yield hops, (s // 2 + (hops if j % 2 == 1 else ring - hops)) % ring * 2

    def attend_near(step, f):
        rows = [flat(recv[step, 0, :, pl.ds(low, 2)]) for _, low in origins(f)]
        rows = jnp.concatenate(rows, axis=0).astype(jnp.float32) * HEAD_DIM**-0.5
        queries[step, f] = jnp.concatenate(
            [jnp.where(first, rows, 0.0), jnp.where(first, 0.0, rows)], axis=0
        ).astype(jnp.bfloat16)
        high, numer, total = weigh(step, f, 0, context_start, None)
        tops[step, f] = jnp.broadcast_to(high, (2 * block_rows, LANES))
        numers[step, f] = numer
        totals[step, f] = total

    def attend_context(step, f):
        top = tops[step, f]
        high, numer, total = weigh(step, f, context_start, 2 * ctx_rows, top[:, :1])
        scale = jnp.exp(top - high)
        left, right = scale[:block_rows], scale[block_rows:]
        numer = numer + numers[step, f] * jnp.where(first, left, right)
        total = total + totals[step, f] * jnp.where(first, right, left)
        total = pltpu.roll(total, HEAD_DIM, 1)
        mixed = numer / total
        for m, (_, low) in enumerate(origins(f)):
            rows = mixed[m * part_rows : (m + 1) * part_rows]
            done[step, :, pl.ds(low, 2)] = rows.reshape(frames, 2, 8, LANES).astype(jnp.bfloat16)

    def landing(step):
        return out.at[step, :, :, pl.ds(s * LANES, LANES)]

    def own_out(step):
        return pltpu.make_async_copy(done.at[step, :, s], landing(step), own_sem.at[len(groups) + 2 + step])

    def send_out(step, f):
        for hops, low in origins(f):
            for to in (low + (s + 1) % 2, low + s % 2):

                @pl.when(to != s)
                def _():
                    remote(done.at[step, :, to], landing(step), out_send.at[step], out_recv.at[step], c, to)

    def send_edges():
        wait_group(1)

        @pl.when(c < clips - 1)
        def _():
            remote(
                recv.at[0, pl.ds(1, 2), frames - 1], edge.at[0], edge_send.at[0], edge_recv.at[0], c + 1, s
            )

        @pl.when(c > 0)
        def _():
            remote(recv.at[0, pl.ds(1, 2), 0], edge.at[1], edge_send.at[1], edge_recv.at[1], c - 1, s)

        @pl.when(c == 0)
        def _():
            edge[0] = jnp.zeros(edge.shape[1:], edge.dtype)

        @pl.when(c == clips - 1)
        def _():
            edge[1] = jnp.zeros(edge.shape[1:], edge.dtype)

    def collect():
        gather(0, ctx)
        gather(1, pooled)

    for copy in small:
        copy.wait()

    after = jnp.minimum(c + 1, clips - 1)
    before_ok = (c > 0) & (cuts[c] == 0)
    after_ok = (c < clips - 1) & (cuts[after] == 0)

    def put_near(step):
        if step == 1:
            wait_group(3)
        put_own(step)
        put_edge(step, before_ok, after_ok)

    def near(step):
        put_near(step)
        wait_group(2 + 2 * step)
        for f in range(blocks):
            attend_near(step, f)

    def finish(step):
        put_context(step)
        for f in range(blocks):
            attend_context(step, f)
            send_out(step, f)
        own_out(step).start()

    def whole(step):
        put_near(step)
        put_context(step)
        wait_group(2 + 2 * step)
        for f in range(blocks):
            attend_near(step, f)
            attend_context(step, f)
            send_out(step, f)
        own_out(step).start()

    def wait_edges():
        @pl.when(c > 0)
        def _():
            wait_bytes(edge.at[0], edge_recv.at[0])

        @pl.when(c < clips - 1)
        def _():
            wait_bytes(edge.at[1], edge_recv.at[1])

    first_planes = z < zs // 4

    @pl.when(first_planes)
    def _():
        send_edges()
        wait_edges()
        near(0)
        collect()
        near(1)

    @pl.when(jnp.logical_not(first_planes | hold))
    def _():
        send_edges()

    @pl.when(jnp.logical_not(first_planes))
    def _():
        collect()

    @pl.when(hold)
    def _():
        send_edges()

    @pl.when(jnp.logical_not(first_planes))
    def _():
        wait_edges()
        near(0)

    finish(0)

    @pl.when(first_planes)
    def _():
        finish(1)

    @pl.when(jnp.logical_not(first_planes))
    def _():
        whole(1)

    for g in range(len(groups)):
        wait_bytes(others(groups[g]), in_send.at[g])

    @pl.when(c < clips - 1)
    def _():
        wait_bytes(edge.at[0], edge_send.at[0])

    @pl.when(c > 0)
    def _():
        wait_bytes(edge.at[1], edge_send.at[1])

    for e in range(2):
        wait_bytes(scat[e].at[pl.ds(0, clips - 1)], ex_send.at[e, 0])
        wait_bytes(full[e].at[pl.ds(0, zs - 1)], ex_send.at[e, 1])
    for step in range(2):
        all_but_one = done.at[step, :, pl.ds(0, sps - 1)]
        wait_bytes(all_but_one, out_send.at[step])
        wait_bytes(all_but_one, out_recv.at[step])
        own_out(step).wait()


def on_device(clips, sps, features, context, scene_cuts, key_clips, owner_slot):
    steps, kinds, _, frames, tokens, width = features.shape
    tiles = context.shape[1] * context.shape[2] // 8
    zs = clips // QUAD
    part = tiles // zs
    frame_rows = sps * 8
    blocks = sps // 2 // max(sps // 8, 1)
    block_rows = frames * frame_rows // blocks
    key_rows = (frames + 2) * frame_rows + tiles * 8
    dma = pltpu.SemaphoreType.DMA
    half = jnp.bfloat16
    anywhere = pl.BlockSpec(memory_space=pltpu.HBM)
    mixed = pl.pallas_call(
        functools.partial(kernel, clips, sps),
        out_shape=pltpu.VMEM((steps, frames, tokens, width), half),
        in_specs=[anywhere] * 5,
        out_specs=pl.BlockSpec(memory_space=pltpu.VMEM),
        scratch_shapes=[
            pltpu.VMEM((steps, kinds, frames, sps, 8, LANES), half),
            pltpu.VMEM((2, 2, sps, 8, LANES), half),
            pltpu.VMEM((tiles, 8, LANES), half),
            pltpu.VMEM((clips, part, 8, LANES), half),
            pltpu.VMEM((clips, part, 8, LANES), half),
            pltpu.VMEM((zs, NKEY, part, 8, LANES), half),
            pltpu.VMEM((zs, NKEY, part, 8, LANES), half),
            pltpu.VMEM((2, key_rows, LANES), half),
            pltpu.VMEM((2, 2, key_rows, LANES), half),
            pltpu.VMEM((steps, blocks, 2 * block_rows, LANES), half),
            pltpu.VMEM((steps, blocks, 2 * block_rows, LANES), jnp.float32),
            pltpu.VMEM((steps, blocks, block_rows, LANES), jnp.float32),
            pltpu.VMEM((steps, blocks, block_rows, LANES), jnp.float32),
            pltpu.VMEM((steps, frames, sps, 8, LANES), half),
            pltpu.SMEM(scene_cuts.shape, jnp.int32),
            pltpu.SMEM(key_clips.shape, jnp.int32),
            pltpu.SMEM((owner_slot.size,), jnp.int32),
            dma((3,)),
            pltpu.SemaphoreType.REGULAR,
            dma((5,)),
            dma((5,)),
            dma((9,)),
            dma((2,)),
            dma((2,)),
            dma((2, 2)),
            dma((2, 2)),
            dma((2,)),
            dma((2,)),
        ],
        compiler_params=pltpu.CompilerParams(
            collective_id=0, has_side_effects=True, vmem_limit_bytes=60 * 2**20
        ),
    )(
        features.reshape(steps, kinds, frames, tokens, width),
        context.reshape(tiles, 8, LANES),
        scene_cuts,
        key_clips,
        owner_slot.reshape(-1),
    )
    return mixed.reshape(steps, 1, frames, tokens, width)


def solution(mesh):
    placed = (
        P(None, None, "clip", None, "sp", None),
        P("clip", None, None, "sp"),
        P(),
        P(),
        P("clip", None),
    )
    return jax.shard_map(
        functools.partial(on_device, mesh.shape["clip"], mesh.shape["sp"]),
        mesh=mesh,
        in_specs=placed,
        out_specs=P(None, "clip", None, "sp", None),
        check_vma=False,
    )
```

```python
import functools

import jax
import jax.numpy as jnp
from jax import lax
from jax.experimental import pallas as pl
from jax.experimental.pallas import tpu as pltpu
from jax.sharding import PartitionSpec as P

HEAD_DIM = 64
LANES = 128
QUAD = 4
NKEY = 4
MESH = pl.DeviceIdType.MESH


def wait_bytes(ref, sem):
    pltpu.make_async_copy(ref, ref, sem).wait()


def flat(block):
    wide = block.astype(jnp.float32)
    return wide.reshape(-1, LANES).astype(jnp.bfloat16)


def kernel(
    clips,
    sps,
    feat,
    ctx,
    cuts_hbm,
    key_clips_hbm,
    slots_hbm,
    out,
    recv,
    edge,
    pooled,
    scat_0,
    scat_1,
    full_0,
    full_1,
    keys,
    vals,
    queries,
    tops,
    numers,
    totals,
    done,
    cuts,
    key_clips,
    slots,
    index_sem,
    above_sem,
    in_send,
    in_recv,
    own_sem,
    edge_send,
    edge_recv,
    ex_send,
    ex_recv,
    out_send,
    out_recv,
):
    c = lax.axis_index("clip")
    s = lax.axis_index("sp")
    zs = clips // QUAD
    z = c // QUAD
    q = c % QUAD
    frames = recv.shape[2]
    tiles = ctx.shape[0]
    part = tiles // zs
    frame_rows = sps * 8
    own_rows = frames * frame_rows
    ctx_rows = tiles * 4
    scat, full = (scat_0, scat_1), (full_0, full_1)

    small = [
        pltpu.make_async_copy(src, dst, index_sem.at[i])
        for i, (src, dst) in enumerate(((cuts_hbm, cuts), (key_clips_hbm, key_clips), (slots_hbm, slots)))
    ]

    ring = sps // 2

    def partner(j, across):
        hops = ring // 2 - (j + 1) // 2
        y = (s // 2 + jnp.where(j % 2 == 1, hops, ring - hops)) % ring
        return y * 2 + (s + across) % 2

    barrier = pltpu.get_barrier_semaphore()

    def greet(clip, sp):
        pl.semaphore_signal(barrier, inc=1, device_id=(clip, sp), device_id_type=MESH)

    def greet_clip(clip, _):
        greet(clip, s)
        return 0

    def greet_quad(k, _):
        greet(z * QUAD + (q + k) % QUAD, s)
        return 0

    for across in (1, 0):

        def greet_sp(j, _):
            greet(c, partner(j, across))
            return 0

        lax.fori_loop(0, ring - 1 + across, greet_sp, 0)
    lax.fori_loop(1, QUAD, greet_quad, 0)
    lax.fori_loop((z + 1) * QUAD, clips, greet_clip, 0)
    for copy in small:
        copy.start()
    pl.semaphore_wait(barrier, sps - 1 + QUAD - 1 + z * QUAD)

    def remote(src, dst, send, rcv, clip, sp):
        pltpu.make_async_remote_copy(
            src_ref=src,
            dst_ref=dst,
            send_sem=send,
            recv_sem=rcv,
            device_id=(clip, sp),
            device_id_type=MESH,
        ).start()

    groups = (
        (0, 1, 2, 0, 1),
        (0, 1, 2, 1, frames - 1),
        (0, 0, 1, 0, frames),
        (1, 1, 2, 0, frames),
        (1, 0, 1, 0, frames),
    )

    def block(group, sp):
        step, low, size, start, count = group
        return feat.at[step, pl.ds(low, size), pl.ds(start, count), :, pl.ds(sp * LANES, LANES)]

    def place(group, sp):
        step, low, size, start, count = group
        return recv.at[step, pl.ds(low, size), pl.ds(start, count), sp]

    def others(group):
        step, low, size, start, count = group
        return recv.at[step, pl.ds(low, size), pl.ds(start, count), pl.ds(0, sps - 1)]

    def own_copy(g):
        return pltpu.make_async_copy(block(groups[g], s), place(groups[g], s), own_sem.at[g])

    def send_group(g, across):
        def one(j, _):
            to = partner(j, across)
            remote(block(groups[g], to), place(groups[g], s), in_send.at[g], in_recv.at[g], c, to)
            return 0

        lax.fori_loop(0, ring - 1 + across, one, 0)

    def wait_group(g):
        own_copy(g).wait()
        wait_bytes(others(groups[g]), in_recv.at[g])

    def scatter_own(e, src):
        return pltpu.make_async_copy(
            src.at[pl.ds(z * part, part)], scat[e].at[c], own_sem.at[len(groups) + e]
        )

    def scatter(e, src):
        def one(j, _):
            plane = (z + 1 + j // QUAD) % zs
            remote(
                src.at[pl.ds(plane * part, part)],
                scat[e].at[c],
                ex_send.at[e, 0],
                ex_recv.at[e, 0],
                plane * QUAD + (q + 2 + j % QUAD) % QUAD,
                s,
            )
            return 0

        def near(j, _):
            remote(
                src.at[pl.ds(z * part, part)],
                scat[e].at[c],
                ex_send.at[e, 0],
                ex_recv.at[e, 0],
                z * QUAD + (q + j) % QUAD,
                s,
            )
            return 0

        scatter_own(e, src).start()
        lax.fori_loop(0, clips - QUAD, one, 0, unroll=QUAD)
        lax.fori_loop(1, QUAD, near, 0, unroll=True)

    def gather(e, src):
        scatter_own(e, src).wait()
        wait_bytes(scat[e].at[pl.ds(0, clips - 1)], ex_recv.at[e, 0])
        for i in range(NKEY):
            full[e][z, i] = scat[e][key_clips[i]]

        def one(k, _):
            @pl.when(k != z)
            def _():
                remote(
                    full[e].at[z],
                    full[e].at[z],
                    ex_send.at[e, 1],
                    ex_recv.at[e, 1],
                    k * QUAD + q,
                    s,
                )

            return 0

        lax.fori_loop(0, zs, one, 0)

    for across in (1, 0):
        send_group(0, across)
    for g in range(len(groups)):
        own_copy(g).start()

    def report(clip, _):
        pl.semaphore_signal(above_sem, inc=1, device_id=(clip, s), device_id_type=MESH)
        return 0

    lax.fori_loop(0, z * QUAD, report, 0)

    @pl.when(z == zs - 1)
    def _():
        scatter(0, ctx)

    early = z < zs // 2
    hold = z >= 3 * zs // 4

    @pl.when(jnp.logical_not(hold))
    def _():
        for g in (1, 2):
            send_group(g, 1)
            send_group(g, 0)

    @pl.when(hold)
    def _():
        for g in (1, 2):
            send_group(g, 0)

    for g in (3, 4):
        send_group(g, 0)

    @pl.when(z < 2)
    def _():
        for g in (3, 4):
            send_group(g, 1)

    @pl.when(z < zs - 1)
    def _():
        pl.semaphore_wait(above_sem, (zs - 1 - z) * QUAD)
        scatter(0, ctx)
    wait_group(0)
    half = tiles // 2
    row = lax.broadcasted_iota(jnp.int32, (half * 8, frame_rows), 0)
    col = lax.broadcasted_iota(jnp.int32, (half * 8, frame_rows), 1)
    pairs = ((col == 2 * row) | (col == 2 * row + 1)).astype(jnp.bfloat16)
    for j in range(2):
        added = jnp.dot(pairs, flat(recv[0, 1 + j, 0]), preferred_element_type=jnp.float32)
        pooled[pl.ds(j * half, half)] = (added * 2**-0.5).reshape(half, 8, LANES).astype(jnp.bfloat16)
    scatter(1, pooled)

    @pl.when(hold)
    def _():
        for g in (1, 2):
            send_group(g, 1)

    @pl.when(z >= 2)
    def _():
        for g in (3, 4):
            send_group(g, 1)

    lane = lax.broadcasted_iota(jnp.int32, (1, LANES), 1)
    first = lane < HEAD_DIM

    def put(step, base, key_rows, value_rows, ok=None):
        rows = key_rows.shape[0]
        where = pl.ds(base, rows)
        ones = jnp.ones((rows, LANES), jnp.bfloat16)
        if ok is not None:
            value_rows = jnp.where(ok, value_rows, jnp.zeros_like(value_rows))
            ones = jnp.where(ok, ones, jnp.zeros_like(ones))
        keys[step, where] = key_rows
        vals[step, 0, where] = jnp.where(first, value_rows, ones)
        vals[step, 1, where] = jnp.where(first, ones, value_rows)

    def put_own(step):
        for f in range(frames):
            put(step, f * frame_rows, flat(recv[step, 1, f]), flat(recv[step, 2, f]))

    def put_edge(step, before_ok, after_ok):
        for side, ok in ((0, before_ok), (1, after_ok)):
            own = recv[step, 1, 0].astype(jnp.float32)
            key_rows = jnp.where(ok, edge[side, 0].astype(jnp.float32), own)
            key_rows = key_rows.reshape(-1, LANES).astype(jnp.bfloat16)
            put(step, own_rows + side * frame_rows, key_rows, flat(edge[side, 1]), ok)

    def put_context(step):
        wait_bytes(full[step].at[pl.ds(0, zs - 1)], ex_recv.at[step, 1])
        for i in range(2):
            base = own_rows + 2 * frame_rows + i * ctx_rows
            taken = flat(full[step][:, slots[i]])
            put(step, base, taken[:ctx_rows], taken[ctx_rows:])

    context_start = own_rows + 2 * frame_rows

    def weigh(step, f, low, count, top):
        scores = lax.dot_general(
            queries[step, f],
            keys[step, pl.ds(low, count)],
            (((1,), (1,)), ((), ())),
            preferred_element_type=jnp.float32,
        )
        high = jnp.max(scores, axis=1, keepdims=True)
        if top is not None:
            high = jnp.maximum(high, top)
        weights = jnp.exp(scores - high).astype(jnp.bfloat16)
        where = pl.ds(low, count)
        left = jnp.dot(weights[:block_rows], vals[step, 0, where], preferred_element_type=jnp.float32)
        right = jnp.dot(weights[block_rows:], vals[step, 1, where], preferred_element_type=jnp.float32)
        return high, jnp.where(first, left, right), jnp.where(first, right, left)

    columns = max(ring // 4, 1)
    blocks = ring // columns
    part_rows = 2 * frames * 8
    block_rows = columns * part_rows

    def origins(f):
        for j in range(f * columns, (f + 1) * columns):
            hops = ring // 2 - (j + 1) // 2
            yield hops, (s // 2 + (hops if j % 2 == 1 else ring - hops)) % ring * 2

    def attend_near(step, f):
        rows = [flat(recv[step, 0, :, pl.ds(low, 2)]) for _, low in origins(f)]
        rows = jnp.concatenate(rows, axis=0).astype(jnp.float32) * HEAD_DIM**-0.5
        queries[step, f] = jnp.concatenate(
            [jnp.where(first, rows, 0.0), jnp.where(first, 0.0, rows)], axis=0
        ).astype(jnp.bfloat16)
        high, numer, total = weigh(step, f, 0, context_start, None)
        tops[step, f] = jnp.broadcast_to(high, (2 * block_rows, LANES))
        numers[step, f] = numer
        totals[step, f] = total

    def attend_context(step, f):
        top = tops[step, f]
        high, numer, total = weigh(step, f, context_start, 2 * ctx_rows, top[:, :1])
        scale = jnp.exp(top - high)
        left, right = scale[:block_rows], scale[block_rows:]
        numer = numer + numers[step, f] * jnp.where(first, left, right)
        total = total + totals[step, f] * jnp.where(first, right, left)
        total = pltpu.roll(total, HEAD_DIM, 1)
        mixed = numer / total
        for m, (_, low) in enumerate(origins(f)):
            rows = mixed[m * part_rows : (m + 1) * part_rows]
            done[step, :, pl.ds(low, 2)] = rows.reshape(frames, 2, 8, LANES).astype(jnp.bfloat16)

    def landing(step):
        return out.at[step, :, :, pl.ds(s * LANES, LANES)]

    def own_out(step):
        return pltpu.make_async_copy(done.at[step, :, s], landing(step), own_sem.at[len(groups) + 2 + step])

    def send_out(step, f):
        for hops, low in origins(f):
            for to in (low + (s + 1) % 2, low + s % 2):

                @pl.when(to != s)
                def _():
                    remote(done.at[step, :, to], landing(step), out_send.at[step], out_recv.at[step], c, to)

    def send_edges():
        wait_group(1)

        @pl.when(c < clips - 1)
        def _():
            remote(
                recv.at[0, pl.ds(1, 2), frames - 1], edge.at[0], edge_send.at[0], edge_recv.at[0], c + 1, s
            )

        @pl.when(c > 0)
        def _():
            remote(recv.at[0, pl.ds(1, 2), 0], edge.at[1], edge_send.at[1], edge_recv.at[1], c - 1, s)

        @pl.when(c == 0)
        def _():
            edge[0] = jnp.zeros(edge.shape[1:], edge.dtype)

        @pl.when(c == clips - 1)
        def _():
            edge[1] = jnp.zeros(edge.shape[1:], edge.dtype)

    def collect():
        gather(0, ctx)
        gather(1, pooled)

    for copy in small:
        copy.wait()

    after = jnp.minimum(c + 1, clips - 1)
    before_ok = (c > 0) & (cuts[c] == 0)
    after_ok = (c < clips - 1) & (cuts[after] == 0)

    def put_near(step):
        if step == 1:
            wait_group(3)
        put_own(step)
        put_edge(step, before_ok, after_ok)

    def near(step):
        put_near(step)
        wait_group(2 + 2 * step)
        for f in range(blocks):
            attend_near(step, f)

    def finish(step):
        put_context(step)
        for f in range(blocks):
            attend_context(step, f)
            send_out(step, f)
        own_out(step).start()

    def whole(step):
        put_near(step)
        put_context(step)
        wait_group(2 + 2 * step)
        for f in range(blocks):
            attend_near(step, f)
            attend_context(step, f)
            send_out(step, f)
        own_out(step).start()

    def wait_edges():
        @pl.when(c > 0)
        def _():
            wait_bytes(edge.at[0], edge_recv.at[0])

        @pl.when(c < clips - 1)
        def _():
            wait_bytes(edge.at[1], edge_recv.at[1])

    first_planes = z < zs // 4

    @pl.when(first_planes)
    def _():
        send_edges()
        wait_edges()
        near(0)
        collect()
        near(1)

    @pl.when(jnp.logical_not(first_planes | hold))
    def _():
        send_edges()

    @pl.when(jnp.logical_not(first_planes))
    def _():
        collect()

    @pl.when(hold)
    def _():
        send_edges()

    @pl.when(jnp.logical_not(first_planes))
    def _():
        wait_edges()
        near(0)

    finish(0)

    @pl.when(first_planes)
    def _():
        finish(1)

    @pl.when(jnp.logical_not(first_planes))
    def _():
        whole(1)

    for g in range(len(groups)):
        wait_bytes(others(groups[g]), in_send.at[g])

    @pl.when(c < clips - 1)
    def _():
        wait_bytes(edge.at[0], edge_send.at[0])

    @pl.when(c > 0)
    def _():
        wait_bytes(edge.at[1], edge_send.at[1])

    for e in range(2):
        wait_bytes(scat[e].at[pl.ds(0, clips - 1)], ex_send.at[e, 0])
        wait_bytes(full[e].at[pl.ds(0, zs - 1)], ex_send.at[e, 1])
    for step in range(2):
        all_but_one = done.at[step, :, pl.ds(0, sps - 1)]
        wait_bytes(all_but_one, out_send.at[step])
        wait_bytes(all_but_one, out_recv.at[step])
        own_out(step).wait()


def on_device(clips, sps, features, context, scene_cuts, key_clips, owner_slot):
    steps, kinds, _, frames, tokens, width = features.shape
    tiles = context.shape[1] * context.shape[2] // 8
    zs = clips // QUAD
    part = tiles // zs
    frame_rows = sps * 8
    blocks = sps // 2 // max(sps // 8, 1)
    block_rows = frames * frame_rows // blocks
    key_rows = (frames + 2) * frame_rows + tiles * 8
    dma = pltpu.SemaphoreType.DMA
    half = jnp.bfloat16
    anywhere = pl.BlockSpec(memory_space=pltpu.HBM)
    mixed = pl.pallas_call(
        functools.partial(kernel, clips, sps),
        out_shape=pltpu.VMEM((steps, frames, tokens, width), half),
        in_specs=[anywhere] * 5,
        out_specs=pl.BlockSpec(memory_space=pltpu.VMEM),
        scratch_shapes=[
            pltpu.VMEM((steps, kinds, frames, sps, 8, LANES), half),
            pltpu.VMEM((2, 2, sps, 8, LANES), half),
            pltpu.VMEM((tiles, 8, LANES), half),
            pltpu.VMEM((clips, part, 8, LANES), half),
            pltpu.VMEM((clips, part, 8, LANES), half),
            pltpu.VMEM((zs, NKEY, part, 8, LANES), half),
            pltpu.VMEM((zs, NKEY, part, 8, LANES), half),
            pltpu.VMEM((2, key_rows, LANES), half),
            pltpu.VMEM((2, 2, key_rows, LANES), half),
            pltpu.VMEM((steps, blocks, 2 * block_rows, LANES), half),
            pltpu.VMEM((steps, blocks, 2 * block_rows, LANES), jnp.float32),
            pltpu.VMEM((steps, blocks, block_rows, LANES), jnp.float32),
            pltpu.VMEM((steps, blocks, block_rows, LANES), jnp.float32),
            pltpu.VMEM((steps, frames, sps, 8, LANES), half),
            pltpu.SMEM(scene_cuts.shape, jnp.int32),
            pltpu.SMEM(key_clips.shape, jnp.int32),
            pltpu.SMEM((owner_slot.size,), jnp.int32),
            dma((3,)),
            pltpu.SemaphoreType.REGULAR,
            dma((5,)),
            dma((5,)),
            dma((9,)),
            dma((2,)),
            dma((2,)),
            dma((2, 2)),
            dma((2, 2)),
            dma((2,)),
            dma((2,)),
        ],
        compiler_params=pltpu.CompilerParams(
            collective_id=0, has_side_effects=True, vmem_limit_bytes=60 * 2**20
        ),
    )(
        features.reshape(steps, kinds, frames, tokens, width),
        context.reshape(tiles, 8, LANES),
        scene_cuts,
        key_clips,
        owner_slot.reshape(-1),
    )
    return mixed.reshape(steps, 1, frames, tokens, width)


def solution(mesh):
    placed = (
        P(None, None, "clip", None, "sp", None),
        P("clip", None, None, "sp"),
        P(),
        P(),
        P("clip", None),
    )
    return jax.shard_map(
        functools.partial(on_device, mesh.shape["clip"], mesh.shape["sp"]),
        mesh=mesh,
        in_specs=placed,
        out_specs=P(None, "clip", None, "sp", None),
        check_vma=False,
    )
```

```python
import functools

import jax
import jax.numpy as jnp
from jax import lax
from jax.experimental import pallas as pl
from jax.experimental.pallas import tpu as pltpu
from jax.sharding import PartitionSpec as P

HEAD_DIM = 64
LANES = 128
QUAD = 4
NKEY = 4
MESH = pl.DeviceIdType.MESH


def wait_bytes(ref, sem):
    pltpu.make_async_copy(ref, ref, sem).wait()


def flat(block):
    wide = block.astype(jnp.float32)
    return wide.reshape(-1, LANES).astype(jnp.bfloat16)


def kernel(
    clips,
    sps,
    feat,
    ctx,
    cuts_hbm,
    key_clips_hbm,
    slots_hbm,
    out,
    recv,
    edge,
    pooled,
    scat_0,
    scat_1,
    full_0,
    full_1,
    keys,
    vals,
    queries,
    tops,
    numers,
    totals,
    done,
    cuts,
    key_clips,
    slots,
    index_sem,
    above_sem,
    in_send,
    in_recv,
    own_sem,
    edge_send,
    edge_recv,
    ex_send,
    ex_recv,
    out_send,
    out_recv,
):
    c = lax.axis_index("clip")
    s = lax.axis_index("sp")
    zs = clips // QUAD
    z = c // QUAD
    q = c % QUAD
    frames = recv.shape[2]
    tiles = ctx.shape[0]
    part = tiles // zs
    frame_rows = sps * 8
    own_rows = frames * frame_rows
    ctx_rows = tiles * 4
    scat, full = (scat_0, scat_1), (full_0, full_1)

    small = [
        pltpu.make_async_copy(src, dst, index_sem.at[i])
        for i, (src, dst) in enumerate(((cuts_hbm, cuts), (key_clips_hbm, key_clips), (slots_hbm, slots)))
    ]

    ring = sps // 2

    def partner(j, across):
        hops = ring // 2 - (j + 1) // 2
        y = (s // 2 + jnp.where(j % 2 == 1, hops, ring - hops)) % ring
        return y * 2 + (s + across) % 2

    barrier = pltpu.get_barrier_semaphore()

    def greet(clip, sp):
        pl.semaphore_signal(barrier, inc=1, device_id=(clip, sp), device_id_type=MESH)

    def greet_clip(clip, _):
        greet(clip, s)
        return 0

    def greet_quad(k, _):
        greet(z * QUAD + (q + k) % QUAD, s)
        return 0

    for across in (1, 0):

        def greet_sp(j, _):
            greet(c, partner(j, across))
            return 0

        lax.fori_loop(0, ring - 1 + across, greet_sp, 0)
    lax.fori_loop(1, QUAD, greet_quad, 0)
    lax.fori_loop((z + 1) * QUAD, clips, greet_clip, 0)
    for copy in small:
        copy.start()
    pl.semaphore_wait(barrier, sps - 1 + QUAD - 1 + z * QUAD)

    def remote(src, dst, send, rcv, clip, sp):
        pltpu.make_async_remote_copy(
            src_ref=src,
            dst_ref=dst,
            send_sem=send,
            recv_sem=rcv,
            device_id=(clip, sp),
            device_id_type=MESH,
        ).start()

    groups = (
        (0, 1, 2, 0, 1),
        (0, 1, 2, 1, frames - 1),
        (0, 0, 1, 0, frames),
        (1, 1, 2, 0, frames),
        (1, 0, 1, 0, frames),
    )

    def block(group, sp):
        step, low, size, start, count = group
        return feat.at[step, pl.ds(low, size), pl.ds(start, count), :, pl.ds(sp * LANES, LANES)]

    def place(group, sp):
        step, low, size, start, count = group
        return recv.at[step, pl.ds(low, size), pl.ds(start, count), sp]

    def others(group):
        step, low, size, start, count = group
        return recv.at[step, pl.ds(low, size), pl.ds(start, count), pl.ds(0, sps - 1)]

    def own_copy(g):
        return pltpu.make_async_copy(block(groups[g], s), place(groups[g], s), own_sem.at[g])

    def send_group(g, across):
        def one(j, _):
            to = partner(j, across)
            remote(block(groups[g], to), place(groups[g], s), in_send.at[g], in_recv.at[g], c, to)
            return 0

        lax.fori_loop(0, ring - 1 + across, one, 0)

    def wait_group(g):
        own_copy(g).wait()
        wait_bytes(others(groups[g]), in_recv.at[g])

    def scatter_own(e, src):
        return pltpu.make_async_copy(
            src.at[pl.ds(z * part, part)], scat[e].at[c], own_sem.at[len(groups) + e]
        )

    def scatter(e, src):
        def one(j, _):
            plane = (z + 1 + j // QUAD) % zs
            remote(
                src.at[pl.ds(plane * part, part)],
                scat[e].at[c],
                ex_send.at[e, 0],
                ex_recv.at[e, 0],
                plane * QUAD + (q + 2 + j % QUAD) % QUAD,
                s,
            )
            return 0

        def near(j, _):
            remote(
                src.at[pl.ds(z * part, part)],
                scat[e].at[c],
                ex_send.at[e, 0],
                ex_recv.at[e, 0],
                z * QUAD + (q + j) % QUAD,
                s,
            )
            return 0

        scatter_own(e, src).start()
        lax.fori_loop(0, clips - QUAD, one, 0, unroll=QUAD)
        lax.fori_loop(1, QUAD, near, 0, unroll=True)

    def gather(e, src):
        scatter_own(e, src).wait()
        wait_bytes(scat[e].at[pl.ds(0, clips - 1)], ex_recv.at[e, 0])
        for i in range(NKEY):
            full[e][z, i] = scat[e][key_clips[i]]

        def one(k, _):
            @pl.when(k != z)
            def _():
                remote(
                    full[e].at[z],
                    full[e].at[z],
                    ex_send.at[e, 1],
                    ex_recv.at[e, 1],
                    k * QUAD + q,
                    s,
                )

            return 0

        lax.fori_loop(0, zs, one, 0, unroll=True)

    for across in (1, 0):
        send_group(0, across)
    for g in range(len(groups)):
        own_copy(g).start()

    def report(clip, _):
        pl.semaphore_signal(above_sem, inc=1, device_id=(clip, s), device_id_type=MESH)
        return 0

    lax.fori_loop(0, z * QUAD, report, 0)

    @pl.when(z == zs - 1)
    def _():
        scatter(0, ctx)

    early = z < zs // 2
    hold = z >= 3 * zs // 4

    @pl.when(jnp.logical_not(hold))
    def _():
        for g in (1, 2):
            send_group(g, 1)
            send_group(g, 0)

    @pl.when(hold)
    def _():
        for g in (1, 2):
            send_group(g, 0)

    for g in (3, 4):
        send_group(g, 0)

    @pl.when(z < 2)
    def _():
        for g in (3, 4):
            send_group(g, 1)

    @pl.when(z < zs - 1)
    def _():
        pl.semaphore_wait(above_sem, (zs - 1 - z) * QUAD)
        scatter(0, ctx)
    wait_group(0)
    half = tiles // 2
    row = lax.broadcasted_iota(jnp.int32, (half * 8, frame_rows), 0)
    col = lax.broadcasted_iota(jnp.int32, (half * 8, frame_rows), 1)
    pairs = ((col == 2 * row) | (col == 2 * row + 1)).astype(jnp.bfloat16)
    for j in range(2):
        added = jnp.dot(pairs, flat(recv[0, 1 + j, 0]), preferred_element_type=jnp.float32)
        pooled[pl.ds(j * half, half)] = (added * 2**-0.5).reshape(half, 8, LANES).astype(jnp.bfloat16)
    scatter(1, pooled)

    @pl.when(hold)
    def _():
        for g in (1, 2):
            send_group(g, 1)

    @pl.when(z >= 2)
    def _():
        for g in (3, 4):
            send_group(g, 1)

    lane = lax.broadcasted_iota(jnp.int32, (1, LANES), 1)
    first = lane < HEAD_DIM

    def put(step, base, key_rows, value_rows, ok=None):
        rows = key_rows.shape[0]
        where = pl.ds(base, rows)
        ones = jnp.ones((rows, LANES), jnp.bfloat16)
        if ok is not None:
            value_rows = jnp.where(ok, value_rows, jnp.zeros_like(value_rows))
            ones = jnp.where(ok, ones, jnp.zeros_like(ones))
        keys[step, where] = key_rows
        vals[step, 0, where] = jnp.where(first, value_rows, ones)
        vals[step, 1, where] = jnp.where(first, ones, value_rows)

    def put_own(step):
        for f in range(frames):
            put(step, f * frame_rows, flat(recv[step, 1, f]), flat(recv[step, 2, f]))

    def put_edge(step, before_ok, after_ok):
        for side, ok in ((0, before_ok), (1, after_ok)):
            own = recv[step, 1, 0].astype(jnp.float32)
            key_rows = jnp.where(ok, edge[side, 0].astype(jnp.float32), own)
            key_rows = key_rows.reshape(-1, LANES).astype(jnp.bfloat16)
            put(step, own_rows + side * frame_rows, key_rows, flat(edge[side, 1]), ok)

    def put_context(step):
        wait_bytes(full[step].at[pl.ds(0, zs - 1)], ex_recv.at[step, 1])
        for i in range(2):
            base = own_rows + 2 * frame_rows + i * ctx_rows
            taken = flat(full[step][:, slots[i]])
            put(step, base, taken[:ctx_rows], taken[ctx_rows:])

    context_start = own_rows + 2 * frame_rows

    def weigh(step, f, low, count, top):
        scores = lax.dot_general(
            queries[step, f],
            keys[step, pl.ds(low, count)],
            (((1,), (1,)), ((), ())),
            preferred_element_type=jnp.float32,
        )
        high = jnp.max(scores, axis=1, keepdims=True)
        if top is not None:
            high = jnp.maximum(high, top)
        weights = jnp.exp(scores - high).astype(jnp.bfloat16)
        where = pl.ds(low, count)
        left = jnp.dot(weights[:block_rows], vals[step, 0, where], preferred_element_type=jnp.float32)
        right = jnp.dot(weights[block_rows:], vals[step, 1, where], preferred_element_type=jnp.float32)
        return high, jnp.where(first, left, right), jnp.where(first, right, left)

    columns = max(ring // 4, 1)
    blocks = ring // columns
    part_rows = 2 * frames * 8
    block_rows = columns * part_rows

    def origins(f):
        for j in range(f * columns, (f + 1) * columns):
            hops = ring // 2 - (j + 1) // 2
            yield hops, (s // 2 + (hops if j % 2 == 1 else ring - hops)) % ring * 2

    def attend_near(step, f):
        rows = [flat(recv[step, 0, :, pl.ds(low, 2)]) for _, low in origins(f)]
        rows = jnp.concatenate(rows, axis=0).astype(jnp.float32) * HEAD_DIM**-0.5
        queries[step, f] = jnp.concatenate(
            [jnp.where(first, rows, 0.0), jnp.where(first, 0.0, rows)], axis=0
        ).astype(jnp.bfloat16)
        high, numer, total = weigh(step, f, 0, context_start, None)
        tops[step, f] = jnp.broadcast_to(high, (2 * block_rows, LANES))
        numers[step, f] = numer
        totals[step, f] = total

    def attend_context(step, f):
        top = tops[step, f]
        high, numer, total = weigh(step, f, context_start, 2 * ctx_rows, top[:, :1])
        scale = jnp.exp(top - high)
        left, right = scale[:block_rows], scale[block_rows:]
        numer = numer + numers[step, f] * jnp.where(first, left, right)
        total = total + totals[step, f] * jnp.where(first, right, left)
        total = pltpu.roll(total, HEAD_DIM, 1)
        mixed = numer / total
        for m, (_, low) in enumerate(origins(f)):
            rows = mixed[m * part_rows : (m + 1) * part_rows]
            done[step, :, pl.ds(low, 2)] = rows.reshape(frames, 2, 8, LANES).astype(jnp.bfloat16)

    def landing(step):
        return out.at[step, :, :, pl.ds(s * LANES, LANES)]

    def own_out(step):
        return pltpu.make_async_copy(done.at[step, :, s], landing(step), own_sem.at[len(groups) + 2 + step])

    def send_out(step, f):
        for hops, low in origins(f):
            for to in (low + (s + 1) % 2, low + s % 2):

                @pl.when(to != s)
                def _():
                    remote(done.at[step, :, to], landing(step), out_send.at[step], out_recv.at[step], c, to)

    def send_edges():
        wait_group(1)

        @pl.when(c < clips - 1)
        def _():
            remote(
                recv.at[0, pl.ds(1, 2), frames - 1], edge.at[0], edge_send.at[0], edge_recv.at[0], c + 1, s
            )

        @pl.when(c > 0)
        def _():
            remote(recv.at[0, pl.ds(1, 2), 0], edge.at[1], edge_send.at[1], edge_recv.at[1], c - 1, s)

        @pl.when(c == 0)
        def _():
            edge[0] = jnp.zeros(edge.shape[1:], edge.dtype)

        @pl.when(c == clips - 1)
        def _():
            edge[1] = jnp.zeros(edge.shape[1:], edge.dtype)

    def collect():
        gather(0, ctx)
        gather(1, pooled)

    for copy in small:
        copy.wait()

    after = jnp.minimum(c + 1, clips - 1)
    before_ok = (c > 0) & (cuts[c] == 0)
    after_ok = (c < clips - 1) & (cuts[after] == 0)

    def put_near(step):
        if step == 1:
            wait_group(3)
        put_own(step)
        put_edge(step, before_ok, after_ok)

    def near(step):
        put_near(step)
        wait_group(2 + 2 * step)
        for f in range(blocks):
            attend_near(step, f)

    def finish(step):
        put_context(step)
        for f in range(blocks):
            attend_context(step, f)
            send_out(step, f)
        own_out(step).start()

    def whole(step):
        put_near(step)
        put_context(step)
        wait_group(2 + 2 * step)
        for f in range(blocks):
            attend_near(step, f)
            attend_context(step, f)
            send_out(step, f)
        own_out(step).start()

    def wait_edges():
        @pl.when(c > 0)
        def _():
            wait_bytes(edge.at[0], edge_recv.at[0])

        @pl.when(c < clips - 1)
        def _():
            wait_bytes(edge.at[1], edge_recv.at[1])

    first_planes = z < zs // 4

    @pl.when(first_planes)
    def _():
        send_edges()
        wait_edges()
        near(0)
        collect()
        near(1)

    @pl.when(jnp.logical_not(first_planes | hold))
    def _():
        send_edges()

    @pl.when(jnp.logical_not(first_planes))
    def _():
        collect()

    @pl.when(hold)
    def _():
        send_edges()

    @pl.when(jnp.logical_not(first_planes))
    def _():
        wait_edges()
        near(0)

    finish(0)

    @pl.when(first_planes)
    def _():
        finish(1)

    @pl.when(jnp.logical_not(first_planes))
    def _():
        whole(1)

    for g in range(len(groups)):
        wait_bytes(others(groups[g]), in_send.at[g])

    @pl.when(c < clips - 1)
    def _():
        wait_bytes(edge.at[0], edge_send.at[0])

    @pl.when(c > 0)
    def _():
        wait_bytes(edge.at[1], edge_send.at[1])

    for e in range(2):
        wait_bytes(scat[e].at[pl.ds(0, clips - 1)], ex_send.at[e, 0])
        wait_bytes(full[e].at[pl.ds(0, zs - 1)], ex_send.at[e, 1])
    for step in range(2):
        all_but_one = done.at[step, :, pl.ds(0, sps - 1)]
        wait_bytes(all_but_one, out_send.at[step])
        wait_bytes(all_but_one, out_recv.at[step])
        own_out(step).wait()


def on_device(clips, sps, features, context, scene_cuts, key_clips, owner_slot):
    steps, kinds, _, frames, tokens, width = features.shape
    tiles = context.shape[1] * context.shape[2] // 8
    zs = clips // QUAD
    part = tiles // zs
    frame_rows = sps * 8
    blocks = sps // 2 // max(sps // 8, 1)
    block_rows = frames * frame_rows // blocks
    key_rows = (frames + 2) * frame_rows + tiles * 8
    dma = pltpu.SemaphoreType.DMA
    half = jnp.bfloat16
    anywhere = pl.BlockSpec(memory_space=pltpu.HBM)
    mixed = pl.pallas_call(
        functools.partial(kernel, clips, sps),
        out_shape=pltpu.VMEM((steps, frames, tokens, width), half),
        in_specs=[anywhere] * 5,
        out_specs=pl.BlockSpec(memory_space=pltpu.VMEM),
        scratch_shapes=[
            pltpu.VMEM((steps, kinds, frames, sps, 8, LANES), half),
            pltpu.VMEM((2, 2, sps, 8, LANES), half),
            pltpu.VMEM((tiles, 8, LANES), half),
            pltpu.VMEM((clips, part, 8, LANES), half),
            pltpu.VMEM((clips, part, 8, LANES), half),
            pltpu.VMEM((zs, NKEY, part, 8, LANES), half),
            pltpu.VMEM((zs, NKEY, part, 8, LANES), half),
            pltpu.VMEM((2, key_rows, LANES), half),
            pltpu.VMEM((2, 2, key_rows, LANES), half),
            pltpu.VMEM((steps, blocks, 2 * block_rows, LANES), half),
            pltpu.VMEM((steps, blocks, 2 * block_rows, LANES), jnp.float32),
            pltpu.VMEM((steps, blocks, block_rows, LANES), jnp.float32),
            pltpu.VMEM((steps, blocks, block_rows, LANES), jnp.float32),
            pltpu.VMEM((steps, frames, sps, 8, LANES), half),
            pltpu.SMEM(scene_cuts.shape, jnp.int32),
            pltpu.SMEM(key_clips.shape, jnp.int32),
            pltpu.SMEM((owner_slot.size,), jnp.int32),
            dma((3,)),
            pltpu.SemaphoreType.REGULAR,
            dma((5,)),
            dma((5,)),
            dma((9,)),
            dma((2,)),
            dma((2,)),
            dma((2, 2)),
            dma((2, 2)),
            dma((2,)),
            dma((2,)),
        ],
        compiler_params=pltpu.CompilerParams(
            collective_id=0, has_side_effects=True, vmem_limit_bytes=60 * 2**20
        ),
    )(
        features.reshape(steps, kinds, frames, tokens, width),
        context.reshape(tiles, 8, LANES),
        scene_cuts,
        key_clips,
        owner_slot.reshape(-1),
    )
    return mixed.reshape(steps, 1, frames, tokens, width)


def solution(mesh):
    placed = (
        P(None, None, "clip", None, "sp", None),
        P("clip", None, None, "sp"),
        P(),
        P(),
        P("clip", None),
    )
    return jax.shard_map(
        functools.partial(on_device, mesh.shape["clip"], mesh.shape["sp"]),
        mesh=mesh,
        in_specs=placed,
        out_specs=P(None, "clip", None, "sp", None),
        check_vma=False,
    )
```
